256 devices in a mesh: lat: 16 (over y_hi, x, core), lon: 16 (over z, y_lo).
Axes of the slice: x: 4, y: 4 (y_hi: 2, y_lo: 2; y = y_hi * 2 + y_lo), z: 8, core: 2. Of those that a mesh axis runs over, the one named last changes fastest.
Arguments:
- tokens: bfloat16 [2, 192, 384, 192], P(None, 'lat', 'lon'), may hold values from -6 to 6
- w_qkv: bfloat16 [192, 576], replicated, may hold values from -0.4375 to 0.4375
- w_proj: bfloat16 [192, 192], replicated, may hold values from -0.4375 to 0.4375
- w_up: bfloat16 [192, 768], replicated, may hold values from -0.4375 to 0.4375
- w_down: bfloat16 [768, 192], replicated, may hold values from -0.21875 to 0.21875
- earth_bias: float32 [16, 1, 6, 24, 552], P('lat'), may hold values from -2 to 400
- cotangent: bfloat16 [2, 192, 384, 192], P(None, 'lat', 'lon'), may hold values from -6 to 6
Outputs:
- result: bfloat16 [2, 192, 384, 192], P(None, 'lat', 'lon')
- grad_tokens: bfloat16 [2, 192, 384, 192], P(None, 'lat', 'lon')
- grad_qkv: float32 [192, 576], replicated
- grad_proj: float32 [192, 192], replicated
- grad_up: float32 [192, 768], replicated
- grad_down: float32 [768, 192], replicated
- grad_bias: float32 [16, 1, 6, 24, 552], P('lat')
The draws below stay inside these ranges and needn't reach their ends.
All inputs are finite; a program needn't handle non-finite values.
Results may differ from the reference program's by a relative error of at most 0.029.
Values may be sent and summed in bfloat16 or wider, within the bound.
No kernel may reach another device: no remote copies, remote signals or barrier semaphores. Data moves between devices by JAX's collectives and lax.ppermute only.
A program may use at most 128 MiB of HBM per device.

```python
import math
from functools import partial
import jax
import jax.numpy as jnp
from jax import lax

C = 192
HEADS = 6
HID = 768
WZ = 2
WA = 12
WO = 12
LEVELS = 2
LAT = 192
LON = 384
LATW = 16
LEVW = 1
POS = 24
SPAN = 23


def draw_earth_bias(key, part):
    key = jax.random.fold_in(key, 11)
    shape = (LATW, LEVW, HEADS, POS, POS * SPAN)
    return 0.5 * jnp.clip(jax.random.normal(key, shape, jnp.float32), -4.0, 4.0)


def block_scale(own_key, shape, cuts, smallest, largest):
    gain, own = 1.0, jax.random.fold_in(own_key, 6)
    for position, blocks in cuts:
        heights = jnp.exp(jax.random.uniform(jax.random.fold_in(own, position), (blocks,), jnp.float32, smallest / len(cuts), largest / len(cuts)))
        gain = gain * jnp.repeat(heights, shape[position] // blocks).reshape([-1 if axis == position else 1 for axis in range(len(shape))])
    return gain


def normal_values(key, shape, scale, most, cuts=(), kind=jnp.bfloat16):
    values = jax.random.normal(key, shape, jnp.float32) * scale
    if len(cuts) > 0:
        values = block_scale(key, shape, cuts, -0.22, 0.18) * values
    return jnp.clip(values, min=-most, max=most).astype(kind)


def setup_inputs(seed: int = 0) -> dict:
    key_of = jax.random.split(jax.random.key(seed), 8)
    tokens = normal_values(key_of[0], (LEVELS, LAT, LON, C), 1.0, 6.0, ((1, 16), (2, 16)))
    w_qkv = normal_values(key_of[1], (C, 3 * C), C ** -0.5, 0.4375)
    w_proj = normal_values(key_of[2], (C, C), C ** -0.5, 0.4375)
    w_up = normal_values(key_of[3], (C, HID), C ** -0.5, 0.4375)
    w_down = normal_values(key_of[4], (HID, C), HID ** -0.5, 0.21875)
    earth_bias = draw_earth_bias(jax.random.fold_in(key_of[7], 71), 0)
    cotangent = normal_values(key_of[6], (LEVELS, LAT, LON, C), 1.0, 6.0, ((1, 16), (2, 16)))
    return dict(tokens=tokens, w_qkv=w_qkv, w_proj=w_proj, w_up=w_up, w_down=w_down, earth_bias=earth_bias, cotangent=cotangent)


def normalize(values):
    average = lax.optimization_barrier(jnp.mean(values, axis=-1, keepdims=True))
    centred = values - average
    variance = lax.optimization_barrier(jnp.mean(centred * centred, axis=-1, keepdims=True))
    return centred * lax.rsqrt(variance + 1e-05)

def exact_gelu(values):
    return jax.nn.gelu(values, approximate=False)

def offset_table(window):
    row_index = jnp.arange(window)[:, None, None]
    col_index = jnp.arange(window)[None, :, None]
    offsets = jnp.arange(2 * window - 1)[None, None, :]
    return (offsets == row_index - col_index + window - 1).astype(jnp.float32)

def region_codes(band, bands, levwins, depth_count, row_count, col_count):
    level_win = jnp.arange(levwins)[:, None, None, None]
    level_pos = jnp.arange(depth_count)[None, :, None, None]
    row_pos = jnp.arange(row_count)[None, None, :, None]
    zone_level = jnp.where(level_win == levwins - 1, level_pos + 1, 0)
    zone_row = jnp.where(band == bands - 1, (row_pos >= row_count // 2).astype(jnp.int32) + 1, 0)
    codes = zone_level * 3 + zone_row + jnp.zeros((1, 1, 1, col_count), jnp.int32)
    return codes.reshape(levwins, depth_count * row_count * col_count).astype(jnp.int32)

def window_core(packed, table, region):
    levwins, lonwins, window_len, triple = packed.shape
    width = triple // 3
    heads_count = table.shape[1]
    head_size = width // heads_count
    positions = table.shape[2]
    spread = table.shape[3] // positions
    parts = packed.astype(jnp.float32).reshape(levwins, lonwins, window_len, 3, heads_count, head_size)
    queries = parts[:, :, :, 0]
    key_rows = parts[:, :, :, 1]
    value_rows = parts[:, :, :, 2]
    scores = jnp.einsum('lnihd,lnjhd->lnhij', queries, key_rows) * head_size ** (-0.5)
    biases = jnp.einsum('lhpqs,abs->lhpaqb', table.reshape(levwins, heads_count, positions, positions, spread), offset_table((spread + 1) // 2), precision=lax.Precision.HIGHEST)
    scores = scores + biases.reshape(levwins, heads_count, window_len, window_len)[:, None]
    same_region = region[:, :, None] == region[:, None, :]
    scores = jnp.where(same_region[:, None, None], scores, -1e+30)
    maxima = lax.stop_gradient(lax.optimization_barrier(jnp.max(scores, axis=-1, keepdims=True)))
    exponent = jnp.exp(scores - maxima)
    probability = (exponent / lax.optimization_barrier(jnp.sum(exponent, axis=-1, keepdims=True))).astype(jnp.bfloat16)
    attended = jnp.einsum('lnhij,lnjhd->lnihd', probability.astype(jnp.float32), value_rows)
    return attended.reshape(levwins, lonwins, window_len, width).astype(jnp.bfloat16)

def split_windows(block):
    levels, lat_count, lon_count, width = block.shape
    shaped = block.reshape(levels // WZ, WZ, lat_count // WA, WA, lon_count // WO, WO, width)
    return shaped.transpose(2, 0, 4, 1, 3, 5, 6).reshape(lat_count // WA, levels // WZ, lon_count // WO, WZ * WA * WO, width)

def join_windows(windows, levels, lat_count, lon_count):
    width = windows.shape[-1]
    shaped = windows.reshape(lat_count // WA, levels // WZ, lon_count // WO, WZ, WA, WO, width)
    return shaped.transpose(1, 3, 0, 4, 2, 5, 6).reshape(levels, lat_count, lon_count, width)

def reference(tokens, w_qkv, w_proj, w_up, w_down, earth_bias, cotangent):
    levels, lat_count, lon_count, width = tokens.shape
    hidden_width = w_up.shape[1]
    bands = lat_count // WA
    shifts = (-1, -(WA // 2), -(WO // 2))
    backs = (1, WA // 2, WO // 2)
    inputs = tokens.astype(jnp.float32)
    normed = normalize(inputs).astype(jnp.bfloat16)
    windows = split_windows(jnp.roll(normed, shifts, axis=(0, 1, 2)))
    packed = jnp.dot(windows, w_qkv, preferred_element_type=jnp.float32).astype(jnp.bfloat16)
    band_ids = jnp.arange(bands, dtype=jnp.int32)

    def forward_band(operands):
        band_packed, band_table, band = operands
        return window_core(band_packed, band_table, region_codes(band, bands, levels // WZ, WZ, WA, WO))
    attended = lax.map(forward_band, (packed, earth_bias, band_ids))
    mixed = jnp.dot(attended, w_proj, preferred_element_type=jnp.float32).astype(jnp.bfloat16)
    placed = jnp.roll(join_windows(mixed, levels, lat_count, lon_count), backs, axis=(0, 1, 2))
    residual = inputs + placed.astype(jnp.float32)
    normed_two = normalize(residual).astype(jnp.bfloat16)
    upper = jnp.dot(normed_two, w_up, preferred_element_type=jnp.float32)
    activated, gelu_back = jax.vjp(exact_gelu, upper)
    activated = activated.astype(jnp.bfloat16)
    result = (residual + jnp.dot(activated, w_down, preferred_element_type=jnp.float32)).astype(jnp.bfloat16)
    grad_down = jnp.dot(activated.reshape(-1, hidden_width).T, cotangent.reshape(-1, width), preferred_element_type=jnp.float32)
    grad_act = jnp.dot(cotangent, w_down.T, preferred_element_type=jnp.float32).astype(jnp.bfloat16)
    grad_upper = gelu_back(grad_act.astype(jnp.float32))[0].astype(jnp.bfloat16)
    grad_up = jnp.dot(normed_two.reshape(-1, width).T, grad_upper.reshape(-1, hidden_width), preferred_element_type=jnp.float32)
    grad_normed_two = jnp.dot(grad_upper, w_up.T, preferred_element_type=jnp.float32).astype(jnp.bfloat16)
    grad_residual = cotangent.astype(jnp.float32) + jax.vjp(normalize, residual)[1](grad_normed_two.astype(jnp.float32))[0]
    grad_mixed = split_windows(jnp.roll(grad_residual.astype(jnp.bfloat16), shifts, axis=(0, 1, 2)))
    grad_proj = jnp.dot(attended.reshape(-1, width).T, grad_mixed.reshape(-1, width), preferred_element_type=jnp.float32)
    grad_attended = jnp.dot(grad_mixed, w_proj.T, preferred_element_type=jnp.float32).astype(jnp.bfloat16)

    def backward_band(operands):
        band_packed, band_table, band, band_grad = operands
        region = region_codes(band, bands, levels // WZ, WZ, WA, WO)
        core_back = jax.vjp(partial(window_core, region=region), band_packed, band_table)[1]
        return core_back(band_grad)
    grad_packed, grad_table = lax.map(backward_band, (packed, earth_bias, band_ids, grad_attended))
    grad_qkv = jnp.dot(windows.reshape(-1, width).T, grad_packed.reshape(-1, 3 * width), preferred_element_type=jnp.float32)
    grad_windows = jnp.dot(grad_packed, w_qkv.T, preferred_element_type=jnp.float32).astype(jnp.bfloat16)
    grad_normed = jnp.roll(join_windows(grad_windows, levels, lat_count, lon_count), backs, axis=(0, 1, 2))
    grad_tokens = (grad_residual + jax.vjp(normalize, inputs)[1](grad_normed.astype(jnp.float32))[0]).astype(jnp.bfloat16)
    square_total = jnp.sum(grad_qkv * grad_qkv) + jnp.sum(grad_proj * grad_proj) + jnp.sum(grad_up * grad_up) + jnp.sum(grad_down * grad_down)
    count = w_qkv.size + w_proj.size + w_up.size + w_down.size + earth_bias.size
    factor = jnp.minimum(1.0, math.sqrt(count) / (jnp.sqrt(square_total) + 1e-06))
    return (result, grad_tokens, grad_qkv * factor, grad_proj * factor, grad_up * factor, grad_down * factor, grad_table * factor)
```

```python
from functools import partial
import math

import jax
import jax.numpy as jnp
from jax import lax
from jax.sharding import PartitionSpec as P

WZ = 2
WA = 12
WO = 12
LANES = 128


def shifted(block, axis, distance):
    devices = range(lax.axis_size(axis))
    route = [((i - distance) % len(devices), i) for i in devices]
    return lax.ppermute(block, axis, route)


def normalize(values):
    average = jnp.mean(values, axis=-1, keepdims=True)
    centred = values - average
    variance = jnp.mean(centred * centred, axis=-1, keepdims=True)
    return centred * lax.rsqrt(variance + 1e-05)


def exact_gelu(values):
    return jax.nn.gelu(values, approximate=False)


def offset_table(window):
    row_index = jnp.arange(window)[:, None, None]
    col_index = jnp.arange(window)[None, :, None]
    offsets = jnp.arange(2 * window - 1)[None, None, :]
    return (offsets == row_index - col_index + window - 1).astype(jnp.float32)


def region_codes(band, bands, levwins, depth_count, row_count, col_count):
    level_win = jnp.arange(levwins)[:, None, None, None]
    level_pos = jnp.arange(depth_count)[None, :, None, None]
    row_pos = jnp.arange(row_count)[None, None, :, None]
    zone_level = jnp.where(level_win == levwins - 1, level_pos + 1, 0)
    zone_row = jnp.where(band == bands - 1, (row_pos >= row_count // 2).astype(jnp.int32) + 1, 0)
    codes = zone_level * 3 + zone_row + jnp.zeros((1, 1, 1, col_count), jnp.int32)
    return codes.reshape(levwins, depth_count * row_count * col_count)


def window_core(packed, table, region):
    levwins, lonwins, window_len, triple = packed.shape
    width = triple // 3
    heads_count = table.shape[1]
    head_size = width // heads_count
    positions = table.shape[2]
    spread = table.shape[3] // positions
    parts = packed.reshape(levwins, lonwins, window_len, 3, heads_count, head_size)
    queries = parts[:, :, :, 0]
    key_rows = parts[:, :, :, 1]
    value_rows = parts[:, :, :, 2]
    scores = jnp.einsum(
        "lnihd,lnjhd->lnhij", queries, key_rows, preferred_element_type=jnp.float32
    ) * head_size ** (-0.5)
    biases = jnp.einsum(
        "lhpqs,abs->lhpaqb",
        table.reshape(levwins, heads_count, positions, positions, spread),
        offset_table((spread + 1) // 2),
        precision=lax.Precision.HIGHEST,
    )
    scores = scores + biases.reshape(levwins, heads_count, window_len, window_len)[:, None]
    same_region = region[:, :, None] == region[:, None, :]
    scores = jnp.where(same_region[:, None, None], scores, -1e30)
    maxima = lax.stop_gradient(jnp.max(scores, axis=-1, keepdims=True))
    exponent = jnp.exp(scores - maxima)
    probability = (exponent / jnp.sum(exponent, axis=-1, keepdims=True)).astype(jnp.bfloat16)
    attended = jnp.einsum(
        "lnhij,lnjhd->lnihd", probability, value_rows, preferred_element_type=jnp.float32
    )
    return attended.reshape(levwins, lonwins, window_len, width).astype(jnp.bfloat16)


def to_windows(block):
    levels, row_count, col_count, width = block.shape
    shaped = block.reshape(levels // WZ, WZ, row_count, col_count // WO, WO, width)
    return shaped.transpose(0, 3, 1, 2, 4, 5).reshape(
        levels // WZ, col_count // WO, WZ * row_count * WO, width
    )


def from_windows(windows, levels, col_count):
    width = windows.shape[-1]
    shaped = windows.reshape(levels // WZ, col_count // WO, WZ, WA, WO, width)
    return shaped.transpose(0, 2, 3, 1, 4, 5).reshape(levels, WA, col_count, width)


def roll_forward(stacked):
    half_row = WA // 2
    half_col = WO // 2
    arrived = shifted(stacked[:, :, :half_row], "lat", -1)
    stacked = jnp.concatenate([stacked[:, :, half_row:], arrived], axis=2)
    arrived = shifted(stacked[:, :, :, :half_col], "lon", -1)
    stacked = jnp.concatenate([stacked[:, :, :, half_col:], arrived], axis=3)
    return jnp.roll(stacked, -1, axis=1)


def roll_back(stacked):
    half_row = WA // 2
    half_col = WO // 2
    arrived = shifted(stacked[:, :, -half_row:], "lat", 1)
    stacked = jnp.concatenate([arrived, stacked[:, :, :-half_row]], axis=2)
    arrived = shifted(stacked[:, :, :, -half_col:], "lon", 1)
    stacked = jnp.concatenate([arrived, stacked[:, :, :, :-half_col]], axis=3)
    return jnp.roll(stacked, 1, axis=1)


def lanes_of(flat, blocks, rows):
    padded = jnp.pad(flat, (0, blocks * rows * LANES - flat.size))
    return padded.reshape(blocks, rows, LANES)


def all_sums(weights, table):
    lat = lax.axis_size("lat")
    lon = lax.axis_size("lon")
    half = lat // 2
    pairs = [(i, i ^ 1) for i in range(lat)]
    groups = [[2 * i + core for i in range(half)] for core in range(2)]
    core = lax.axis_index("lat") % 2
    rows = -(-weights.size // (lat * LANES))
    rows = -(-rows // 8) * 8
    parts = lanes_of(weights, lat, rows).reshape(2, half, rows, LANES)
    mine = lax.dynamic_index_in_dim(parts, core, 0, keepdims=False)
    other = lax.dynamic_index_in_dim(parts, 1 - core, 0, keepdims=False)
    mine = mine + lax.ppermute(other.astype(jnp.bfloat16), "lat", pairs).astype(jnp.float32)
    got = lax.all_to_all(mine.astype(jnp.bfloat16), "lat", 0, 0, axis_index_groups=groups)
    mine = jnp.sum(got.astype(jnp.float32), axis=0)
    small = -(-rows // (16 * lon)) * 16
    mine = lanes_of(mine.reshape(-1), lon, small)
    share = -(-table.size // (16 * lon * LANES)) * 16
    both = jnp.concatenate([mine, lanes_of(table.reshape(-1), lon, share)], axis=1)
    got = lax.all_to_all(both.astype(jnp.bfloat16), "lon", 0, 0)
    both = jnp.sum(got.astype(jnp.float32), axis=0).astype(jnp.bfloat16)
    got = lax.all_to_all(jnp.broadcast_to(both, (lon,) + both.shape), "lon", 0, 0)
    table_sum = got[:, small:].reshape(-1)[: table.size].reshape(table.shape)
    mine = got[:, :small].reshape(-1, LANES)[:rows]
    got = lax.all_to_all(
        jnp.broadcast_to(mine, (half,) + mine.shape), "lat", 0, 0, axis_index_groups=groups
    )
    other = lax.ppermute(got, "lat", pairs)
    first = jnp.where(core == 0, got, other)
    second = jnp.where(core == 0, other, got)
    whole = jnp.concatenate([first, second], axis=0).reshape(-1)[: weights.size]
    return whole.astype(jnp.float32), table_sum.astype(jnp.float32)


def on_device(tokens, w_qkv, w_proj, w_up, w_down, earth_bias, cotangent):
    band = lax.axis_index("lat")
    bands = lax.axis_size("lat")
    levels, row_count, col_count, width = tokens.shape
    hidden_width = w_up.shape[1]
    table = earth_bias[0]
    region = region_codes(band, bands, levels // WZ, WZ, row_count, WO)
    inputs = tokens.astype(jnp.float32)
    normed = normalize(inputs).astype(jnp.bfloat16)
    rolled = roll_forward(normed[None])[0]
    windows = to_windows(rolled)
    packed = jnp.dot(windows, w_qkv, preferred_element_type=jnp.float32).astype(jnp.bfloat16)
    attended, core_back = jax.vjp(partial(window_core, region=region), packed, table)
    mixed = jnp.dot(attended, w_proj, preferred_element_type=jnp.float32).astype(jnp.bfloat16)
    placed = from_windows(mixed, levels, col_count)
    placed = roll_back(placed[None])[0]
    residual = inputs + placed.astype(jnp.float32)
    normed_two = normalize(residual).astype(jnp.bfloat16)
    upper = jnp.dot(normed_two, w_up, preferred_element_type=jnp.float32)
    activated, gelu_back = jax.vjp(exact_gelu, upper)
    activated = activated.astype(jnp.bfloat16)
    result = (residual + jnp.dot(activated, w_down, preferred_element_type=jnp.float32)).astype(
        jnp.bfloat16
    )
    grad_down = jnp.dot(
        activated.reshape(-1, hidden_width).T,
        cotangent.reshape(-1, width),
        preferred_element_type=jnp.float32,
    )
    grad_act = jnp.dot(cotangent, w_down.T, preferred_element_type=jnp.float32).astype(jnp.bfloat16)
    grad_upper = gelu_back(grad_act.astype(jnp.float32))[0].astype(jnp.bfloat16)
    grad_up = jnp.dot(
        normed_two.reshape(-1, width).T,
        grad_upper.reshape(-1, hidden_width),
        preferred_element_type=jnp.float32,
    )
    grad_normed_two = jnp.dot(grad_upper, w_up.T, preferred_element_type=jnp.float32).astype(
        jnp.bfloat16
    )
    grad_residual = (
        cotangent.astype(jnp.float32)
        + jax.vjp(normalize, residual)[1](grad_normed_two.astype(jnp.float32))[0]
    )
    grad_placed = grad_residual.astype(jnp.bfloat16)
    grad_placed = roll_forward(grad_placed[None])[0]
    grad_mixed = to_windows(grad_placed)
    grad_proj = jnp.dot(
        attended.reshape(-1, width).T,
        grad_mixed.reshape(-1, width),
        preferred_element_type=jnp.float32,
    )
    grad_attended = jnp.dot(grad_mixed, w_proj.T, preferred_element_type=jnp.float32).astype(
        jnp.bfloat16
    )
    grad_packed, grad_table = core_back(grad_attended)
    grad_qkv = jnp.dot(
        windows.reshape(-1, width).T,
        grad_packed.reshape(-1, 3 * width),
        preferred_element_type=jnp.float32,
    )
    grad_windows = jnp.dot(grad_packed, w_qkv.T, preferred_element_type=jnp.float32).astype(
        jnp.bfloat16
    )
    grad_normed = from_windows(grad_windows, levels, col_count)
    grad_normed = roll_back(grad_normed[None])[0]
    grad_tokens = (
        grad_residual + jax.vjp(normalize, inputs)[1](grad_normed.astype(jnp.float32))[0]
    ).astype(jnp.bfloat16)
    grads = (grad_qkv, grad_proj, grad_up, grad_down)
    flat = jnp.concatenate([grad.reshape(-1) for grad in grads])
    flat, table_sum = all_sums(flat, grad_table)
    sums, start = [], 0
    for grad in grads:
        sums.append(flat[start : start + grad.size].reshape(grad.shape))
        start += grad.size
    qkv_sum, proj_sum, up_sum, down_sum = sums
    square_total = jnp.sum(flat * flat)
    count = w_qkv.size + w_proj.size + w_up.size + w_down.size + table.size * bands
    factor = jnp.minimum(1.0, math.sqrt(count) / (jnp.sqrt(square_total) + 1e-06))
    return (
        result,
        grad_tokens,
        qkv_sum * factor,
        proj_sum * factor,
        up_sum * factor,
        down_sum * factor,
        (table_sum * factor)[None],
    )


def solution(mesh):
    placed = (
        P(None, "lat", "lon", None),
        P(),
        P(),
        P(),
        P(),
        P("lat", None, None, None, None),
        P(None, "lat", "lon", None),
    )
    return jax.shard_map(
        on_device,
        mesh=mesh,
        in_specs=placed,
        out_specs=(
            P(None, "lat", "lon", None),
            P(None, "lat", "lon", None),
            P(),
            P(),
            P(),
            P(),
            P("lat", None, None, None, None),
        ),
        check_vma=False,
    )
```

```python
import functools
import math

import jax
import jax.numpy as jnp
import numpy as np
from jax import lax
from jax.experimental import pallas as pl
from jax.experimental.pallas import tpu as pltpu
from jax.sharding import PartitionSpec as P

WA = 12
WO = 12
HALF = 6
HEADS = 6
HEAD = 32
WIN = WA * WO
SPAN = 2 * WO - 1
CUT = WA * SPAN
WIDE = 384
LANES = 128
C = 192
HID = 768
TOKENS = 576
PARTS = 4
PACKED = 1792
EPS = 1e-05
SCALE = HEAD ** (-0.5)
VMEM = 48 * 1024 * 1024
BF = jnp.bfloat16
F32 = jnp.float32


def table_order():
    lane = np.arange(CUT)
    order = np.zeros((CUT, WIDE), np.float32)
    order[(lane % WA) * SPAN + SPAN - 1 - lane // WA, lane] = 1.0
    return order


def table_back():
    back = np.zeros((2, WIDE, 2 * CUT), np.float32)
    for level in range(2):
        back[level, :, level * CUT : (level + 1) * CUT] = table_order().T
    return back


def dot(a, b):
    return jnp.dot(a, b, preferred_element_type=F32)


def dot_rt(a, b):
    return lax.dot_general(a, b, (((1,), (1,)), ((), ())), preferred_element_type=F32)


def dot_lt(a, b):
    return lax.dot_general(a, b, (((0,), (0,)), ((), ())), preferred_element_type=F32)


def normal(values):
    centred = values - jnp.mean(values, axis=-1, keepdims=True)
    variance = jnp.mean(centred * centred, axis=-1, keepdims=True)
    inverse = lax.rsqrt(variance + EPS)
    return centred * inverse, inverse


def normal_back(unit, inverse, grad):
    first = jnp.mean(grad, axis=-1, keepdims=True)
    second = jnp.mean(grad * unit, axis=-1, keepdims=True)
    return inverse * (grad - first - unit * second)


def bias_kernel(last_ref, table_ref, order_ref, bias_ref):
    order = order_ref[...]
    table = table_ref[...]
    high = table.astype(BF)
    rest = table - high.astype(F32)
    middle = rest.astype(BF)
    low = (rest - middle.astype(F32)).astype(BF)
    wide = dot(high, order) + (dot(middle, order) + dot(low, order))
    row = lax.broadcasted_iota(jnp.int32, (2 * WA, WIDE), 0)
    row_i = lax.broadcasted_iota(jnp.int32, (2 * WA, WIN), 0) % WA
    row_j = lax.broadcasted_iota(jnp.int32, (2 * WA, WIN), 1) % WA
    split = (row_i >= HALF) != (row_j >= HALF)
    split = jnp.logical_and(split, last_ref[0] == 1)
    for level in range(2):
        for head in range(HEADS):
            at = (level * HEADS + head) * 2 * WA
            both = wide[at : at + 2 * WA]
            both = jnp.where(row < WA, pltpu.roll(both, WIDE - WA, 1), both)
            for pair in range(WO // 2):
                turn = (WO - 2 - 2 * pair) * WA
                block = pltpu.roll(both, (WIDE - turn) % WIDE, 1)[:, :WIN]
                start = head * WIN + pair * 2 * WA
                bias_ref[level, start : start + 2 * WA, :] = jnp.where(split, -1e30, block)


def block_kernel(
    core_ref, x_ref, cot_ref, wq_ref, wk_ref, wv_ref, proj_ref, up_ref, down_ref, bias_ref,
    result_ref, gtok_ref, mine_ref, other_ref, gbias_ref,
    normed_ref, q_ref, k_ref, v_ref, prob_ref, att_ref, res_ref, two_ref, upper_ref, gact_ref, act_ref,
    gup_ref, gres_ref, gmix_ref, gatt_ref, dq_ref, dk_ref, dv_ref, ds_ref,
):
    lane = lax.broadcasted_iota(jnp.int32, (1, C), 1) // HEAD
    masks = [(lane == head).astype(F32) for head in range(HEADS)]
    half_masks = [mask.astype(BF) for mask in masks]

    def rows_of(part):
        return pl.ds(pl.multiple_of(part * WIN, WIN), WIN)

    def first_norm(part, carry):
        rows = rows_of(part)
        unit, _ = normal(x_ref[rows, :].astype(F32))
        normed_ref[rows, :] = unit.astype(BF)
        return carry

    lax.fori_loop(0, PARTS, first_norm, 0)
    normed = normed_ref[...]
    q_ref[...] = dot(normed, wq_ref[...]).astype(BF)
    k_ref[...] = dot(normed, wk_ref[...]).astype(BF)
    v_ref[...] = dot(normed, wv_ref[...]).astype(BF)

    def attend(part, carry):
        rows = rows_of(part)
        query, key, value = q_ref[rows, :], k_ref[rows, :], v_ref[rows, :]
        level = part % 2
        total = jnp.zeros((WIN, C), F32)
        for head in range(HEADS):
            chunk = slice(head * WIN, (head + 1) * WIN)
            scores = dot_rt(query * half_masks[head], key) * SCALE + bias_ref[level, chunk, :]
            exponent = jnp.exp(scores - jnp.max(scores, axis=-1, keepdims=True))
            prob = exponent / jnp.sum(exponent, axis=-1, keepdims=True)
            prob = prob.astype(BF)
            prob_ref[part, chunk, :] = prob
            total = total + dot(prob, value) * masks[head]
        att_ref[rows, :] = total.astype(BF)
        return carry

    lax.fori_loop(0, PARTS, attend, 0)
    res_ref[...] = dot(att_ref[...], proj_ref[...])

    def second_norm(part, carry):
        rows = rows_of(part)
        residual = x_ref[rows, :].astype(F32) + res_ref[rows, :].astype(BF).astype(F32)
        res_ref[rows, :] = residual
        unit, _ = normal(residual)
        two_ref[rows, :] = unit.astype(BF)
        return carry

    lax.fori_loop(0, PARTS, second_norm, 0)
    upper_ref[...] = dot(two_ref[...], up_ref[...])
    gact_ref[...] = dot_rt(cot_ref[...], down_ref[...]).astype(BF)
    step = 32

    def gelu(chunk, carry):
        rows = pl.ds(pl.multiple_of(chunk * step, step), step)
        upper = upper_ref[rows, :]
        cdf = 0.5 + 0.5 * lax.erf(upper * math.sqrt(0.5))
        pdf = jnp.exp(upper * upper * -0.5) * (1.0 / math.sqrt(2.0 * math.pi))
        act_ref[rows, :] = (upper * cdf).astype(BF)
        gup_ref[rows, :] = (gact_ref[rows, :].astype(F32) * (cdf + upper * pdf)).astype(BF)
        return carry

    lax.fori_loop(0, TOKENS // step, gelu, 0)
    result_ref[...] = (res_ref[...] + dot(act_ref[...], down_ref[...])).astype(BF)
    gres_ref[...] = dot_rt(gup_ref[...], up_ref[...])

    def second_back(part, carry):
        rows = rows_of(part)
        unit, inverse = normal(res_ref[rows, :])
        grad = gres_ref[rows, :].astype(BF).astype(F32)
        grad = cot_ref[rows, :].astype(F32) + normal_back(unit, inverse, grad)
        gres_ref[rows, :] = grad
        gmix_ref[rows, :] = grad.astype(BF)
        return carry

    lax.fori_loop(0, PARTS, second_back, 0)
    gatt_ref[...] = dot_rt(gmix_ref[...], proj_ref[...]).astype(BF)
    ds_ref[...] = jnp.zeros(ds_ref.shape, F32)

    def attend_back(part, carry):
        rows = rows_of(part)
        query, key, value = q_ref[rows, :], k_ref[rows, :], v_ref[rows, :]
        gatt = gatt_ref[rows, :]
        level = part % 2
        gquery = jnp.zeros((WIN, C), F32)
        gkey = jnp.zeros((WIN, C), F32)
        gvalue = jnp.zeros((WIN, C), F32)
        for head in range(HEADS):
            chunk = slice(head * WIN, (head + 1) * WIN)
            prob = prob_ref[part, chunk, :]
            own = gatt * half_masks[head]
            gprob = dot_rt(own, value)
            weight = prob.astype(F32)
            gscore = weight * (gprob - jnp.sum(weight * gprob, axis=-1, keepdims=True))
            ds_ref[level, chunk, :WIN] += gscore
            gscore = (gscore * SCALE).astype(BF)
            gquery = gquery + dot(gscore, key) * masks[head]
            gkey = gkey + dot_lt(gscore, query * half_masks[head])
            gvalue = gvalue + dot_lt(prob, own)
        dq_ref[rows, :] = gquery.astype(BF)
        dk_ref[rows, :] = gkey.astype(BF)
        dv_ref[rows, :] = gvalue.astype(BF)
        return carry

    lax.fori_loop(0, PARTS, attend_back, 0)
    normed_grad = dot_rt(dq_ref[...], wq_ref[...])
    normed_grad = normed_grad + dot_rt(dk_ref[...], wk_ref[...])
    res_ref[...] = normed_grad + dot_rt(dv_ref[...], wv_ref[...])

    def first_back(part, carry):
        rows = rows_of(part)
        unit, inverse = normal(x_ref[rows, :].astype(F32))
        grad = res_ref[rows, :].astype(BF).astype(F32)
        gtok_ref[rows, :] = (gres_ref[rows, :] + normal_back(unit, inverse, grad)).astype(BF)
        return carry

    lax.fori_loop(0, PARTS, first_back, 0)
    first = core_ref[0] == 0

    def put(start, zero, one):
        rows = slice(start, start + zero.shape[0])
        mine_ref[rows, :] = jnp.where(first, zero, one)
        other_ref[rows, :] = jnp.where(first, one, zero).astype(BF)

    gup = dot_lt(two_ref[...], gup_ref[...])
    gdown = dot_lt(act_ref[...], cot_ref[...])
    for chunk in range(4):
        put(chunk * C, gup[:, chunk * LANES : (chunk + 1) * LANES], gdown[chunk * C : (chunk + 1) * C, :LANES])
    for chunk in range(4, 6):
        left = (chunk - 4) * C
        pair = jnp.concatenate([gdown[left : left + C, LANES:], gdown[2 * C + left : 3 * C + left, LANES:]], axis=1)
        put(chunk * C, gup[:, chunk * LANES : (chunk + 1) * LANES], pair)
    normed = normed_ref[...]
    gq = dot_lt(normed, dq_ref[...])
    gk = dot_lt(normed, dk_ref[...])
    gv = dot_lt(normed, dv_ref[...])
    gproj = dot_lt(att_ref[...], gmix_ref[...])
    put(6 * C, gq[:, :LANES], gproj[:, :LANES])
    put(7 * C, gk[:, :LANES], jnp.concatenate([gq[:, LANES:], gk[:, LANES:]], axis=1))
    put(8 * C, gv[:, :LANES], jnp.concatenate([gv[:, LANES:], gproj[:, LANES:]], axis=1))
    mine_ref[9 * C :, :] = jnp.zeros((PACKED - 9 * C, LANES), F32)
    other_ref[9 * C :, :] = jnp.zeros((PACKED - 9 * C, LANES), BF)

    row = lax.broadcasted_iota(jnp.int32, (2 * WA, WIDE), 0)
    for level in range(2):
        for head in range(HEADS):
            total = jnp.zeros((2 * WA, WIDE), F32)
            for pair in range(WO // 2):
                start = head * WIN + pair * 2 * WA
                turn = (WO - 2 - 2 * pair) * WA
                block = ds_ref[level, start : start + 2 * WA, :]
                total = total + (pltpu.roll(block, turn, 1) if turn else block)
            total = jnp.where(row < WA, pltpu.roll(total, WA, 1), total)
            total = total + pltpu.roll(total, WA, 0)
            gbias_ref[level * HEADS + head] = total[:16].astype(BF)
    gbias_ref[2 * HEADS :] = jnp.zeros((16 - 2 * HEADS, 16, WIDE), BF)


def final_kernel(
    count, core_ref, mine_ref, other_ref, gbias_ref, back_ref,
    qkv_ref, proj_ref, up_ref, down_ref, bias_ref,
):
    first = core_ref[0] == 0
    mine = mine_ref[...].astype(F32)
    other = other_ref[...].astype(F32)
    total = jnp.sum(mine * mine) + jnp.sum(other * other)
    factor = jnp.minimum(1.0, math.sqrt(count) / (jnp.sqrt(jnp.full((8, LANES), total)) + 1e-06))[:1]
    zero = jnp.where(first, mine, other) * factor
    one = jnp.where(first, other, mine) * factor

    def chunk(half, place):
        return half[place * C : (place + 1) * C]

    for place in range(6):
        up_ref[:, place * LANES : (place + 1) * LANES] = chunk(zero, place)
    down_ref[:, :LANES] = one[: 4 * C]
    down_ref[: 2 * C, LANES:] = one[4 * C : 6 * C, : C - LANES]
    down_ref[2 * C :, LANES:] = one[4 * C : 6 * C, C - LANES :]
    last = C - LANES
    left, right = chunk(one, 7), chunk(one, 8)
    qkv_ref[:, :C] = jnp.concatenate([chunk(zero, 6), left[:, :last]], axis=1)
    qkv_ref[:, C : 2 * C] = jnp.concatenate([chunk(zero, 7), left[:, last:]], axis=1)
    qkv_ref[:, 2 * C :] = jnp.concatenate([chunk(zero, 8), right[:, :last]], axis=1)
    proj_ref[...] = jnp.concatenate([chunk(one, 6), right[:, last:]], axis=1)
    for level in range(2):
        rows = gbias_ref[level * HEADS : (level + 1) * HEADS].reshape(HEADS * 16, WIDE)
        table = dot(rows, back_ref[level]) * factor[:, :1]
        for head in range(HEADS):
            bias_ref[head, level * WA : (level + 1) * WA, :] = table[head * 16 : head * 16 + WA]


def call(kernel, outs, scalars, arrays, scratch=()):
    spaces = [pl.BlockSpec(memory_space=pltpu.SMEM)] * scalars
    spaces += [pl.BlockSpec(memory_space=pltpu.VMEM)] * arrays
    return pl.pallas_call(
        kernel,
        out_shape=outs,
        in_specs=spaces,
        out_specs=[pl.BlockSpec(memory_space=pltpu.VMEM)] * len(outs),
        scratch_shapes=scratch,
        compiler_params=pltpu.CompilerParams(vmem_limit_bytes=VMEM),
    )


def shape(*sizes, kind=F32):
    return jax.ShapeDtypeStruct(sizes, kind)


def from_next(block, axes, distance):
    sizes = [lax.axis_size(axis) for axis in axes]
    route = []
    for place in np.ndindex(*sizes):
        source = [(i + distance) % size for i, size in zip(place, sizes)]
        route.append((int(np.ravel_multi_index(source, sizes)), int(np.ravel_multi_index(place, sizes))))
    return lax.ppermute(block, tuple(axes), route)


def rolled_windows(pair):
    own, beside = pair[:, :, HALF:, HALF:], pair[:, :, HALF:, :HALF]
    below, corner = pair[:, :, :HALF, HALF:], pair[:, :, :HALF, :HALF]
    below = from_next(below, ["lat"], 1)
    beside = from_next(beside, ["lon"], 1)
    corner = from_next(corner, ["lat", "lon"], 1)
    upper = jnp.concatenate([own, beside], axis=3)
    lower = jnp.concatenate([below, corner], axis=3)
    whole = jnp.concatenate([upper, lower], axis=2)[:, ::-1]
    whole = whole.reshape(2, 2, WA, 2, WO, C).transpose(0, 3, 1, 4, 2, 5)
    return whole.reshape(2, TOKENS, C)


def rolled_back(pair):
    whole = pair.reshape(2, 2, 2, WO, WA, C).transpose(0, 2, 4, 1, 3, 5)
    whole = whole.reshape(2, 2, WA, 2 * WO, C)[:, ::-1]
    cut = 2 * WO - HALF
    own, beside = whole[:, :, :HALF, :cut], whole[:, :, :HALF, cut:]
    above, corner = whole[:, :, HALF:, :cut], whole[:, :, HALF:, cut:]
    above = from_next(above, ["lat"], -1)
    beside = from_next(beside, ["lon"], -1)
    corner = from_next(corner, ["lat", "lon"], -1)
    upper = jnp.concatenate([corner, above], axis=3)
    lower = jnp.concatenate([beside, own], axis=3)
    return jnp.concatenate([upper, lower], axis=2)


def weight_sums(mine, other):
    lat, lon = lax.axis_size("lat"), lax.axis_size("lon")
    half, depth = lat // 2, lon // 2
    pairs = [(i, i ^ 1) for i in range(lat)]
    planes = [
        [(2 * i + core) * lon + 2 * z + low for i in range(half) for low in range(2)]
        for core in range(2)
        for z in range(depth)
    ]
    columns = [[2 * z + low for z in range(depth)] for low in range(2)]
    mine = mine + lax.ppermute(other, "lat", pairs).astype(F32)
    mine = mine.astype(BF).reshape(lat, PACKED // lat, LANES)
    got = lax.all_to_all(mine, ("lat", "lon"), 0, 0, axis_index_groups=planes)
    part = jnp.sum(got.astype(F32), axis=0).astype(BF)
    got = lax.all_to_all(jnp.broadcast_to(part, (depth,) + part.shape), "lon", 0, 0, axis_index_groups=columns)
    part = jnp.sum(got.astype(F32), axis=0).astype(BF)
    part = jnp.broadcast_to(part, (lat,) + part.shape)
    mine = lax.all_to_all(part, ("lat", "lon"), 0, 0, axis_index_groups=planes)
    other = lax.ppermute(mine, "lat", pairs)
    return mine.reshape(PACKED, LANES), other.reshape(PACKED, LANES)


def bias_sums(table):
    lon = lax.axis_size("lon")
    parts = table.reshape(lon, table.shape[0] // lon, *table.shape[1:])
    got = lax.all_to_all(parts, "lon", 0, 0)
    part = jnp.sum(got.astype(F32), axis=0).astype(BF)
    got = lax.all_to_all(jnp.broadcast_to(part, (lon,) + part.shape), "lon", 0, 0)
    return got.reshape(table.shape)


def on_device(tokens, w_qkv, w_proj, w_up, w_down, earth_bias, cotangent):
    band = lax.axis_index("lat")
    bands = lax.axis_size("lat")
    core = (band % 2).astype(jnp.int32).reshape(1)
    last = (band == bands - 1).astype(jnp.int32).reshape(1)

    windows = rolled_windows(jnp.stack([tokens, cotangent]))
    table = earth_bias.reshape(HEADS, 2, WA, 2, CUT)
    table = jnp.stack([table[:, 0, :, 0], table[:, 1, :, 1]])
    table = jnp.broadcast_to(table[:, :, None], (2, HEADS, 2, WA, CUT)).reshape(-1, CUT)
    order = jnp.asarray(table_order(), BF)
    bias = call(bias_kernel, [shape(2, HEADS * WIN, WIN)], 1, 2)(last, table, order)[0]

    def tokens_of(width, kind=BF):
        return pltpu.VMEM((TOKENS, width), kind)

    outs = [
        shape(TOKENS, C, kind=BF),
        shape(TOKENS, C, kind=BF),
        shape(PACKED, LANES),
        shape(PACKED, LANES, kind=BF),
        shape(16, 16, WIDE, kind=BF),
    ]
    scratch = [tokens_of(C)] * 4 + [pltpu.VMEM((PARTS, HEADS * WIN, WIN), BF), tokens_of(C), tokens_of(C, F32)]
    scratch += [tokens_of(C), tokens_of(HID, F32)] + [tokens_of(HID)] * 3 + [tokens_of(C, F32)]
    scratch += [tokens_of(C)] * 5 + [pltpu.VMEM((2, HEADS * WIN, WIDE), F32)]
    result, grad_tokens, mine, other, grad_table = call(block_kernel, outs, 1, 9, scratch)(
        core, windows[0], windows[1], w_qkv[:, :C], w_qkv[:, C : 2 * C], w_qkv[:, 2 * C :], w_proj, w_up, w_down, bias
    )
    mine, other = weight_sums(mine, other)
    grad_table = bias_sums(grad_table)
    back = rolled_back(jnp.stack([result, grad_tokens]))

    count = w_qkv.size + w_proj.size + w_up.size + w_down.size + earth_bias.size * bands
    outs = [shape(C, 3 * C), shape(C, C), shape(C, HID), shape(HID, C), shape(HEADS, 2 * WA, 2 * CUT)]
    grads = call(functools.partial(final_kernel, count), outs, 1, 4)(
        core, mine, other, grad_table, jnp.asarray(table_back(), BF)
    )
    return (back[0], back[1], *grads[:4], grads[4][None, None])


def solution(mesh):
    placed = (
        P(None, "lat", "lon", None),
        P(),
        P(),
        P(),
        P(),
        P("lat", None, None, None, None),
        P(None, "lat", "lon", None),
    )
    return jax.shard_map(
        on_device,
        mesh=mesh,
        in_specs=placed,
        out_specs=(
            P(None, "lat", "lon", None),
            P(None, "lat", "lon", None),
            P(),
            P(),
            P(),
            P(),
            P("lat", None, None, None, None),
        ),
        check_vma=False,
    )
```

```python
import functools
import math

import jax
import jax.numpy as jnp
import numpy as np
from jax import lax
from jax.experimental import pallas as pl
from jax.experimental.pallas import tpu as pltpu
from jax.sharding import PartitionSpec as P

WA = 12
WO = 12
HALF = 6
HEADS = 6
HEAD = 32
WIN = WA * WO
SPAN = 2 * WO - 1
CUT = WA * SPAN
WIDE = 384
LANES = 128
C = 192
HID = 768
TOKENS = 576
PARTS = 4
PACKED = 1792
SOURCES = 768
MAIN = HEADS * WA
BIAS_ROWS = 176
LEFT = CUT - 2 * LANES
EPS = 1e-05
SCALE = HEAD ** (-0.5)
VMEM = 48 * 1024 * 1024
BF = jnp.bfloat16
F32 = jnp.float32


def table_order():
    lane = np.arange(CUT)
    order = np.zeros((CUT, WIDE), np.float32)
    order[(lane % WA) * SPAN + SPAN - 1 - lane // WA, lane] = 1.0
    return order


def table_back():
    back = np.zeros((2, WIDE, 2 * CUT), np.float32)
    for level in range(2):
        back[level, :, level * CUT : (level + 1) * CUT] = table_order().T
    return back


def window_order():
    order = np.zeros((TOKENS, SOURCES), np.float32)
    near, far = 2 * HALF * 2 * WO, 2 * HALF * 8
    for window, level, column, row in np.ndindex(2, 2, WO, WA):
        token = ((window * 2 + level) * WO + column) * WA + row
        place, across = (1 - level) * HALF + row % HALF, window * WO + column + HALF
        inside = across < 2 * WO
        at = place * 2 * WO + across if inside else 2 * near + place * 8 + across - 2 * WO
        if row >= HALF:
            at += near if inside else far
        order[token, at] = 1.0
    return order


def dot(a, b):
    return jnp.dot(a, b, preferred_element_type=F32)


def dot_rt(a, b):
    return lax.dot_general(a, b, (((1,), (1,)), ((), ())), preferred_element_type=F32)


def dot_lt(a, b):
    return lax.dot_general(a, b, (((0,), (0,)), ((), ())), preferred_element_type=F32)


def row_mean(values, exact=False):
    ones = jnp.full((C, C), 1.0, BF)
    high = values.astype(BF)
    total = dot(high, ones)
    if not exact:
        total = total + dot((values - high.astype(F32)).astype(BF), ones)
    return total * (1.0 / C)


def normal(values, mean):
    centred = values - mean
    inverse = lax.rsqrt(row_mean(centred * centred) + EPS)
    return centred * inverse, inverse


def normal_back(unit, inverse, grad):
    first = row_mean(grad, exact=True)
    second = row_mean(grad * unit)
    return inverse * (grad - first - unit * second)


def halo_kernel(tokens_ref, cot_ref, below_ref, beside_ref, corner_ref):
    for array, ref in enumerate((tokens_ref, cot_ref)):
        for level in range(2):
            for row in range(HALF):
                below_ref[array, level, row] = ref[level, row]
                beside_ref[array, level, row] = ref[level, row + HALF].astype(F32)[:8].astype(BF)
                corner_ref[array, level, row] = ref[level, row].astype(F32)[:8].astype(BF)


def bias_kernel(last_ref, table_ref, order_ref, bias_ref):
    order = order_ref[...]
    table = table_ref[...]
    high = table.astype(BF)
    rest = table - high.astype(F32)
    middle = rest.astype(BF)
    low = (rest - middle.astype(F32)).astype(BF)
    wide = dot(high, order) + (dot(middle, order) + dot(low, order))
    row = lax.broadcasted_iota(jnp.int32, (2 * WA, WIDE), 0)
    row_i = lax.broadcasted_iota(jnp.int32, (2 * WA, WIN), 0) % WA
    row_j = lax.broadcasted_iota(jnp.int32, (2 * WA, WIN), 1) % WA
    split = (row_i >= HALF) != (row_j >= HALF)
    split = jnp.logical_and(split, last_ref[0] == 1)
    for level in range(2):
        for head in range(HEADS):
            at = (level * HEADS + head) * 2 * WA
            both = wide[at : at + 2 * WA]
            both = jnp.where(row < WA, pltpu.roll(both, WIDE - WA, 1), both)
            blocks = []
            for pair in range(WO // 2):
                turn = (WO - 2 - 2 * pair) * WA
                block = pltpu.roll(both, (WIDE - turn) % WIDE, 1)[:, :WIN]
                blocks.append(jnp.where(split, -1e30, block))
            block = jnp.transpose(jnp.concatenate(blocks, axis=0))
            bias_ref[level, head * WIN : (head + 1) * WIN, :] = block


def block_kernel(
    core_ref, low_ref, tokens_ref, cots_ref, below_ref, beside_ref, corner_ref, order_ref,
    wq_ref, wk_ref, wv_ref, proj_ref, up_ref, down_ref, bias_ref,
    result_ref, gtok_ref, mine_ref, other_ref, bmine_ref, bother_ref,
    source_ref, x_ref, cot_ref, bsum_ref, normed_ref, q_ref, k_ref, v_ref, prob_ref, att_ref, res_ref, two_ref, upper_ref, gact_ref, act_ref,
    gup_ref, gres_ref, gmix_ref, gatt_ref, dq_ref, dk_ref, dv_ref, ds_ref, pad_ref, turned_ref,
    unit_ref, inverse_ref, unit_two_ref, inverse_two_ref, mean_ref,
):
    lane = lax.broadcasted_iota(jnp.int32, (1, C), 1) // HEAD
    half_masks = [(lane == head).astype(F32).astype(BF) for head in range(HEADS)]

    def rows_of(part):
        return pl.ds(pl.multiple_of(part * WIN, WIN), WIN)

    near, far = 2 * HALF * 2 * WO, 2 * HALF * 8
    for array, (ref, target) in enumerate(((tokens_ref, x_ref), (cots_ref, cot_ref))):
        for level in range(2):
            for row in range(HALF):
                place = level * HALF + row
                at = place * 2 * WO
                source_ref[at : at + 2 * WO, :] = ref[level, row + HALF].astype(F32)
                source_ref[near + at : near + at + 2 * WO, :] = below_ref[array, level, row].astype(F32)
                at = 2 * near + place * 8
                source_ref[at : at + 8, :] = beside_ref[array, level, row].astype(F32)
                source_ref[far + at : far + at + 8, :] = corner_ref[array, level, row].astype(F32)
        target[...] = dot(order_ref[...], source_ref[...].astype(BF)).astype(BF)

    def first_norm(part, carry):
        rows = rows_of(part)
        mean = row_mean(x_ref[rows, :], exact=True)
        unit, inverse = normal(x_ref[rows, :].astype(F32), mean)
        mean_ref[rows, :] = mean
        unit_ref[rows, :] = unit
        inverse_ref[rows, :] = inverse
        normed_ref[rows, :] = unit.astype(BF)
        return carry

    lax.fori_loop(0, PARTS, first_norm, 0, unroll=4)
    normed = normed_ref[...]
    q_ref[...] = dot(normed, wq_ref[...]).astype(BF)
    k_ref[...] = dot(normed, wk_ref[...]).astype(BF)
    v_ref[...] = dot(normed, wv_ref[...]).astype(BF)

    def attend(part, carry):
        rows = rows_of(part)
        query, key, value = q_ref[rows, :], k_ref[rows, :], v_ref[rows, :]
        level = part % 2
        value_t = jnp.transpose(value)
        chunks = [slice(head * WIN, (head + 1) * WIN) for head in range(HEADS)]
        scores = [dot_rt(key * mask, query) for mask in half_masks]
        for head, chunk in enumerate(chunks):
            score = scores[head] * SCALE + bias_ref[level, chunk, :]
            exponent = jnp.exp(score - jnp.max(score, axis=0, keepdims=True))
            prob = exponent * (1.0 / jnp.sum(exponent, axis=0, keepdims=True))
            prob_ref[part, chunk, :] = prob.astype(BF)
        for head, chunk in enumerate(chunks):
            own = slice(head * HEAD, (head + 1) * HEAD)
            turned_ref[own, :] = dot(value_t[own], prob_ref[part, chunk, :])
        att_ref[rows, :] = jnp.transpose(turned_ref[...]).astype(BF)
        return carry

    lax.fori_loop(0, PARTS, attend, 0, unroll=4)
    res_ref[...] = dot(att_ref[...], proj_ref[...])

    def second_norm(part, carry):
        rows = rows_of(part)
        mixed = res_ref[rows, :].astype(BF)
        residual = x_ref[rows, :].astype(F32) + mixed.astype(F32)
        res_ref[rows, :] = residual
        unit, inverse = normal(residual, mean_ref[rows, :] + row_mean(mixed, exact=True))
        unit_two_ref[rows, :] = unit
        inverse_two_ref[rows, :] = inverse
        two_ref[rows, :] = unit.astype(BF)
        return carry

    lax.fori_loop(0, PARTS, second_norm, 0, unroll=4)
    upper_ref[...] = dot(two_ref[...], up_ref[...])
    gact_ref[...] = dot(cot_ref[...], down_ref[...]).astype(BF)
    step = 32

    def gelu(chunk, carry):
        rows = pl.ds(pl.multiple_of(chunk * step, step), step)
        upper = upper_ref[rows, :]
        cdf = 0.5 + 0.5 * lax.erf(upper * math.sqrt(0.5))
        pdf = jnp.exp(upper * upper * -0.5) * (1.0 / math.sqrt(2.0 * math.pi))
        act_ref[rows, :] = (upper * cdf).astype(BF)
        gup_ref[rows, :] = (gact_ref[rows, :].astype(F32) * (cdf + upper * pdf)).astype(BF)
        return carry

    lax.fori_loop(0, TOKENS // step, gelu, 0)
    result_ref[...] = (res_ref[...] + dot_rt(act_ref[...], down_ref[...])).astype(BF)
    gres_ref[...] = dot_rt(gup_ref[...], up_ref[...])

    def second_back(part, carry):
        rows = rows_of(part)
        unit, inverse = unit_two_ref[rows, :], inverse_two_ref[rows, :]
        grad = gres_ref[rows, :].astype(BF).astype(F32)
        grad = cot_ref[rows, :].astype(F32) + normal_back(unit, inverse, grad)
        gres_ref[rows, :] = grad
        gmix_ref[rows, :] = grad.astype(BF)
        return carry

    lax.fori_loop(0, PARTS, second_back, 0, unroll=4)
    gatt_ref[...] = dot_rt(gmix_ref[...], proj_ref[...]).astype(BF)
    ds_ref[...] = jnp.zeros(ds_ref.shape, F32)
    pad_ref[...] = jnp.zeros(pad_ref.shape, F32)

    def attend_back(part, carry):
        rows = rows_of(part)
        query, key, value = q_ref[rows, :], k_ref[rows, :], v_ref[rows, :]
        gatt = gatt_ref[rows, :]
        level = part % 2
        key_t = jnp.transpose(key)
        chunks = [slice(head * WIN, (head + 1) * WIN) for head in range(HEADS)]
        gowns = [gatt * mask for mask in half_masks]
        gprobs = [dot_rt(value, gown) for gown in gowns]
        gscores = []
        for head, chunk in enumerate(chunks):
            weight = prob_ref[part, chunk, :].astype(F32)
            gscore = weight * (gprobs[head] - jnp.sum(weight * gprobs[head], axis=0, keepdims=True))
            ds_ref[level, chunk, :] += gscore
            gscores.append(gscore.astype(BF))
        gkey = jnp.zeros((WIN, C), F32)
        gvalue = jnp.zeros((WIN, C), F32)
        for head, chunk in enumerate(chunks):
            own = slice(head * HEAD, (head + 1) * HEAD)
            turned_ref[own, :] = dot(key_t[own], gscores[head])
            gkey = gkey + dot(gscores[head], query * half_masks[head])
            gvalue = gvalue + dot(prob_ref[part, chunk, :], gowns[head])
        dq_ref[rows, :] = (jnp.transpose(turned_ref[...]) * SCALE).astype(BF)
        dk_ref[rows, :] = (gkey * SCALE).astype(BF)
        dv_ref[rows, :] = gvalue.astype(BF)
        return carry

    lax.fori_loop(0, PARTS, attend_back, 0, unroll=4)
    normed_grad = dot_rt(dq_ref[...], wq_ref[...])
    normed_grad = normed_grad + dot_rt(dk_ref[...], wk_ref[...])
    res_ref[...] = normed_grad + dot_rt(dv_ref[...], wv_ref[...])

    def first_back(part, carry):
        rows = rows_of(part)
        unit, inverse = unit_ref[rows, :], inverse_ref[rows, :]
        grad = res_ref[rows, :].astype(BF).astype(F32)
        gtok_ref[rows, :] = (gres_ref[rows, :] + normal_back(unit, inverse, grad)).astype(BF)
        return carry

    lax.fori_loop(0, PARTS, first_back, 0, unroll=4)
    first = core_ref[0] == 0

    def put(start, zero, one):
        rows = slice(start, start + zero.shape[0])
        mine_ref[rows, :] = jnp.where(first, zero, one)
        other_ref[rows, :] = jnp.where(first, one, zero).astype(BF)

    gup = dot_lt(two_ref[...], gup_ref[...])
    gdown = dot_lt(cot_ref[...], act_ref[...])
    for chunk in range(6):
        columns = slice(chunk * LANES, (chunk + 1) * LANES)
        put(chunk * C, gup[:, columns], gdown[:, columns])
    normed = normed_ref[...]
    gq = dot_lt(normed, dq_ref[...])
    gk = dot_lt(normed, dk_ref[...])
    gv = dot_lt(normed, dv_ref[...])
    gproj = dot_lt(att_ref[...], gmix_ref[...])
    put(6 * C, gq[:, :LANES], gproj[:, :LANES])
    put(7 * C, gk[:, :LANES], jnp.concatenate([gq[:, LANES:], gk[:, LANES:]], axis=1))
    put(8 * C, gv[:, :LANES], jnp.concatenate([gv[:, LANES:], gproj[:, LANES:]], axis=1))
    mine_ref[9 * C :, :] = jnp.zeros((PACKED - 9 * C, LANES), F32)
    other_ref[9 * C :, :] = jnp.zeros((PACKED - 9 * C, LANES), BF)

    row = lax.broadcasted_iota(jnp.int32, (2 * WA, WIDE), 0)

    def table_grad(level, head):
        place = level * HEADS + head
        pad_ref[place, :, :WIN] = jnp.transpose(ds_ref[level, head * WIN : (head + 1) * WIN, :])
        total = jnp.zeros((2 * WA, WIDE), F32)
        for pair in range(WO // 2):
            turn = (WO - 2 - 2 * pair) * WA
            block = pad_ref[place, pair * 2 * WA : (pair + 1) * 2 * WA, :]
            total = total + (pltpu.roll(block, turn, 1) if turn else block)
        total = jnp.where(row < WA, pltpu.roll(total, WA, 1), total)
        return total + pltpu.roll(total, WA, 0)

    for level in range(2):
        left = jnp.zeros((2 * WA, LANES), F32)
        for pair in range(HEADS // 2):
            both = jnp.where(row < WA, table_grad(level, 2 * pair), table_grad(level, 2 * pair + 1))
            start = pair * 2 * WA
            bsum_ref[level, start : start + 2 * WA, :] = both[:, :LANES]
            bsum_ref[level, MAIN + start : MAIN + start + 2 * WA, :] = both[:, LANES : 2 * LANES]
            rest = both[:, 2 * LANES :]
            left = left + (pltpu.roll(rest, pair * LEFT, 1) if pair else rest)
        bsum_ref[level, 2 * MAIN : 2 * MAIN + 2 * WA, :] = left
        bsum_ref[level, 2 * MAIN + 2 * WA :, :] = jnp.zeros((BIAS_ROWS - 2 * MAIN - 2 * WA, LANES), F32)
    lower = low_ref[0] == 0
    zero, one = bsum_ref[0], bsum_ref[1]
    bmine_ref[...] = jnp.where(lower, zero, one)
    bother_ref[...] = jnp.where(lower, one, zero).astype(BF)


def final_kernel(
    count, core_ref, low_ref, mine_ref, other_ref, bmine_ref, bother_ref, back_ref,
    qkv_ref, proj_ref, up_ref, down_ref, bias_ref,
):
    first = core_ref[0] == 0
    mine = mine_ref[...].astype(F32)
    other = other_ref[...].astype(F32)
    total = jnp.sum(mine * mine) + jnp.sum(other * other)
    factor = jnp.minimum(1.0, math.sqrt(count) / (jnp.sqrt(jnp.full((8, LANES), total)) + 1e-06))[:1]
    zero = jnp.where(first, mine, other) * factor
    one = jnp.where(first, other, mine) * factor

    def chunk(half, place):
        return half[place * C : (place + 1) * C]

    for place in range(6):
        up_ref[:, place * LANES : (place + 1) * LANES] = chunk(zero, place)
        down_ref[:, place * LANES : (place + 1) * LANES] = chunk(one, place)
    last = C - LANES
    left, right = chunk(one, 7), chunk(one, 8)
    qkv_ref[:, :C] = jnp.concatenate([chunk(zero, 6), left[:, :last]], axis=1)
    qkv_ref[:, C : 2 * C] = jnp.concatenate([chunk(zero, 7), left[:, last:]], axis=1)
    qkv_ref[:, 2 * C :] = jnp.concatenate([chunk(zero, 8), right[:, :last]], axis=1)
    proj_ref[...] = jnp.concatenate([chunk(one, 6), right[:, last:]], axis=1)

    lower = low_ref[0] == 0
    bmine = bmine_ref[...].astype(F32)
    bother = bother_ref[...].astype(F32)
    tables = []
    for level, packed in enumerate((jnp.where(lower, bmine, bother), jnp.where(lower, bother, bmine))):
        left = packed[2 * MAIN : 2 * MAIN + 2 * WA]
        left = [left] + [pltpu.roll(left, LANES - pair * LEFT, 1) for pair in range(1, HEADS // 2)]
        rows = [packed[:MAIN], packed[MAIN : 2 * MAIN], jnp.concatenate(left, axis=0)]
        rows = jnp.concatenate(rows, axis=1).astype(BF)
        tables.append(dot(rows, back_ref[level]) * factor[:, :1])
    row = lax.broadcasted_iota(jnp.int32, (2 * WA, 2 * CUT), 0)
    for pair in range(HEADS // 2):
        upper, lower = [table[pair * 2 * WA : (pair + 1) * 2 * WA] for table in tables]
        bias_ref[0, 0, 2 * pair] = jnp.where(row < WA, upper, pltpu.roll(lower, WA, 0))
        bias_ref[0, 0, 2 * pair + 1] = jnp.where(row < WA, pltpu.roll(upper, WA, 0), lower)


def call(kernel, outs, scalars, arrays, scratch=()):
    spaces = [pl.BlockSpec(memory_space=pltpu.SMEM)] * scalars
    spaces += [pl.BlockSpec(memory_space=pltpu.VMEM)] * arrays
    return pl.pallas_call(
        kernel,
        out_shape=outs,
        in_specs=spaces,
        out_specs=[pl.BlockSpec(memory_space=pltpu.VMEM)] * len(outs),
        scratch_shapes=scratch,
        compiler_params=pltpu.CompilerParams(vmem_limit_bytes=VMEM),
    )


def shape(*sizes, kind=F32):
    return jax.ShapeDtypeStruct(sizes, kind)


def from_next(block, axes, distance):
    sizes = [lax.axis_size(axis) for axis in axes]
    route = []
    for place in np.ndindex(*sizes):
        source = [(i + distance) % size for i, size in zip(place, sizes)]
        route.append((int(np.ravel_multi_index(source, sizes)), int(np.ravel_multi_index(place, sizes))))
    return lax.ppermute(block, tuple(axes), route)


def rolled_back(pair):
    whole = pair.reshape(2, 2, 2, WO, WA, C).transpose(0, 2, 4, 1, 3, 5)
    whole = whole.reshape(2, 2, WA, 2 * WO, C)[:, ::-1]
    cut = 2 * WO - HALF
    own, beside = whole[:, :, :HALF, :cut], whole[:, :, :HALF, cut:]
    above, corner = whole[:, :, HALF:, :cut], whole[:, :, HALF:, cut:]
    above = from_next(above, ["lat"], -1)
    beside = from_next(beside, ["lon"], -1)
    corner = from_next(corner, ["lat", "lon"], -1)
    upper = jnp.concatenate([corner, above], axis=3)
    lower = jnp.concatenate([beside, own], axis=3)
    return jnp.concatenate([upper, lower], axis=2)


def gradient_sums(mine, other, bmine, bother):
    lat, lon = lax.axis_size("lat"), lax.axis_size("lon")
    half, depth = lat // 2, lon // 2
    pairs = [(i, i ^ 1) for i in range(lat)]
    beside = [(i, i ^ 1) for i in range(lon)]
    planes = [
        [(2 * i + core) * lon + 2 * z + low for i in range(half) for low in range(2)]
        for core in range(2)
        for z in range(depth)
    ]
    columns = [[2 * z + low for z in range(depth)] for low in range(2)]
    mine = mine + lax.ppermute(other, "lat", pairs).astype(F32)
    bmine = (bmine + lax.ppermute(bother, "lon", beside).astype(F32)).astype(BF)
    mine = mine.astype(BF).reshape(lat, PACKED // lat, LANES)
    got = lax.all_to_all(mine, ("lat", "lon"), 0, 0, axis_index_groups=planes)
    part = jnp.sum(got.astype(F32), axis=0).astype(BF)
    share = part.shape[0]
    part = jnp.concatenate([part, bmine])
    got = lax.all_to_all(jnp.broadcast_to(part, (depth,) + part.shape), "lon", 0, 0, axis_index_groups=columns)
    part = jnp.sum(got.astype(F32), axis=0).astype(BF)
    part, bmine = part[:share], part[share:]
    bother = lax.ppermute(bmine, "lon", beside)
    part = jnp.broadcast_to(part, (lat,) + part.shape)
    mine = lax.all_to_all(part, ("lat", "lon"), 0, 0, axis_index_groups=planes)
    other = lax.ppermute(mine, "lat", pairs)
    return mine.reshape(PACKED, LANES), other.reshape(PACKED, LANES), bmine, bother


def on_device(tokens, w_qkv, w_proj, w_up, w_down, earth_bias, cotangent):
    band = lax.axis_index("lat")
    bands = lax.axis_size("lat")
    core = (band % 2).astype(jnp.int32).reshape(1)
    low = (lax.axis_index("lon") % 2).astype(jnp.int32).reshape(1)
    last = (band == bands - 1).astype(jnp.int32).reshape(1)

    wide, narrow = shape(2, 2, HALF, 2 * WO, C, kind=BF), shape(2, 2, HALF, 8, C, kind=BF)
    below, beside, corner = call(halo_kernel, [wide, narrow, narrow], 0, 2)(tokens, cotangent)
    below = from_next(below, ["lat"], 1)
    corner = from_next(corner, ["lat", "lon"], 1)
    beside = from_next(beside, ["lon"], 1)
    table = earth_bias.reshape(HEADS, 2, WA, 2, CUT)
    table = jnp.stack([table[:, 0, :, 0], table[:, 1, :, 1]])
    table = jnp.broadcast_to(table[:, :, None], (2, HEADS, 2, WA, CUT)).reshape(-1, CUT)
    order = jnp.asarray(table_order(), BF)
    bias = call(bias_kernel, [shape(2, HEADS * WIN, WIN)], 1, 2)(last, table, order)[0]

    def tokens_of(width, kind=BF):
        return pltpu.VMEM((TOKENS, width), kind)

    outs = [
        shape(TOKENS, C, kind=BF),
        shape(TOKENS, C, kind=BF),
        shape(PACKED, LANES),
        shape(PACKED, LANES, kind=BF),
        shape(BIAS_ROWS, LANES),
        shape(BIAS_ROWS, LANES, kind=BF),
    ]
    scratch = [pltpu.VMEM((SOURCES, C), F32), tokens_of(C), tokens_of(C), pltpu.VMEM((2, BIAS_ROWS, LANES), F32)]
    scratch += [tokens_of(C)] * 4 + [pltpu.VMEM((PARTS, HEADS * WIN, WIN), BF), tokens_of(C), tokens_of(C, F32)]
    scratch += [tokens_of(C), tokens_of(HID, F32)] + [tokens_of(HID)] * 3 + [tokens_of(C, F32)]
    scratch += [tokens_of(C)] * 5 + [pltpu.VMEM((2, HEADS * WIN, WIN), F32)]
    scratch += [pltpu.VMEM((2 * HEADS, WIN, WIDE), F32), pltpu.VMEM((C, WIN), F32)]
    scratch += [tokens_of(C, F32)] * 5
    result, grad_tokens, *grads = call(block_kernel, outs, 2, 13, scratch)(
        core, low, tokens, cotangent, below, beside, corner, jnp.asarray(window_order(), BF),
        w_qkv[:, :C], w_qkv[:, C : 2 * C], w_qkv[:, 2 * C :], w_proj, w_up, w_down.T, bias,
    )
    sums = gradient_sums(*grads)
    back = rolled_back(jnp.stack([result, grad_tokens]))

    count = w_qkv.size + w_proj.size + w_up.size + w_down.size + earth_bias.size * bands
    outs = [shape(C, 3 * C), shape(C, C), shape(C, HID), shape(C, HID), shape(1, 1, HEADS, 2 * WA, 2 * CUT)]
    grads = call(functools.partial(final_kernel, count), outs, 2, 5)(
        core, low, *sums, jnp.asarray(table_back(), BF)
    )
    return (back[0], back[1], *grads[:3], grads[3].T, grads[4])


def solution(mesh):
    placed = (
        P(None, "lat", "lon", None),
        P(),
        P(),
        P(),
        P(),
        P("lat", None, None, None, None),
        P(None, "lat", "lon", None),
    )
    return jax.shard_map(
        on_device,
        mesh=mesh,
        in_specs=placed,
        out_specs=(
            P(None, "lat", "lon", None),
            P(None, "lat", "lon", None),
            P(),
            P(),
            P(),
            P(),
            P("lat", None, None, None, None),
        ),
        check_vma=False,
    )
```

```python
import functools
import math

import jax
import jax.numpy as jnp
import numpy as np
from jax import lax
from jax.experimental import pallas as pl
from jax.experimental.pallas import tpu as pltpu
from jax.sharding import PartitionSpec as P

WA = 12
WO = 12
HALF = 6
HEADS = 6
HEAD = 32
WIN = WA * WO
SPAN = 2 * WO - 1
CUT = WA * SPAN
WIDE = 384
LANES = 128
C = 192
HID = 768
TOKENS = 576
PARTS = 4
PACKED = 1792
SOURCES = 768
MAIN = HEADS * WA
BIAS_ROWS = 176
LEFT = CUT - 2 * LANES
EPS = 1e-05
SCALE = HEAD ** (-0.5)
LARGE = 28 * 1024 * 1024
SMALL = 12 * 1024 * 1024
BF = jnp.bfloat16
F32 = jnp.float32


def table_order():
    lane = np.arange(CUT)
    order = np.zeros((CUT, WIDE), np.float32)
    order[(lane % WA) * SPAN + SPAN - 1 - lane // WA, lane] = 1.0
    return order


def table_back():
    back = np.zeros((2, WIDE, 2 * CUT), np.float32)
    for level in range(2):
        back[level, :, level * CUT : (level + 1) * CUT] = table_order().T
    return back


def window_order():
    order = np.zeros((TOKENS, SOURCES), np.float32)
    near, far = 2 * HALF * 2 * WO, 2 * HALF * 8
    for window, level, column, row in np.ndindex(2, 2, WO, WA):
        token = ((window * 2 + level) * WO + column) * WA + row
        place, across = (1 - level) * HALF + row % HALF, window * WO + column + HALF
        inside = across < 2 * WO
        at = place * 2 * WO + across if inside else 2 * near + place * 8 + across - 2 * WO
        if row >= HALF:
            at += near if inside else far
        order[token, at] = 1.0
    return order


def dot(a, b):
    return jnp.dot(a, b, preferred_element_type=F32)


def dot_rt(a, b):
    return lax.dot_general(a, b, (((1,), (1,)), ((), ())), preferred_element_type=F32)


def dot_lt(a, b):
    return lax.dot_general(a, b, (((0,), (0,)), ((), ())), preferred_element_type=F32)


def row_mean(values, exact=False):
    ones = jnp.full((C, C), 1.0, BF)
    high = values.astype(BF)
    total = dot(high, ones)
    if not exact:
        total = total + dot((values - high.astype(F32)).astype(BF), ones)
    return total * (1.0 / C)


def normal(values, mean):
    centred = values - mean
    inverse = lax.rsqrt(row_mean(centred * centred) + EPS)
    return centred * inverse, inverse


def normal_back(unit, inverse, grad):
    first = row_mean(grad, exact=True)
    second = row_mean(grad * unit)
    return inverse * (grad - first - unit * second)


def halo_kernel(tokens_ref, cot_ref, below_ref, beside_ref, corner_ref):
    for array, ref in enumerate((tokens_ref, cot_ref)):
        for level in range(2):
            for row in range(HALF):
                below_ref[array, level, row] = ref[level, row]
                beside_ref[array, level, row] = ref[level, row + HALF].astype(F32)[:8].astype(BF)
                corner_ref[array, level, row] = ref[level, row].astype(F32)[:8].astype(BF)


def bias_kernel(last_ref, table_ref, order_ref, bias_ref):
    table = table_ref[0, 0].reshape(HEADS * 2 * WA, 2 * CUT)
    high = table.astype(BF)
    rest = table - high.astype(F32)
    middle = rest.astype(BF)
    low = (rest - middle.astype(F32)).astype(BF)
    row = lax.broadcasted_iota(jnp.int32, (2 * WA, WIDE), 0)
    row_i = lax.broadcasted_iota(jnp.int32, (2 * WA, WIN), 0) % WA
    row_j = lax.broadcasted_iota(jnp.int32, (2 * WA, WIN), 1) % WA
    split = (row_i >= HALF) != (row_j >= HALF)
    split = jnp.logical_and(split, last_ref[0] == 1)
    for level in range(2):
        order = order_ref[level]
        wide = dot(high, order) + (dot(middle, order) + dot(low, order))
        for head in range(HEADS):
            both = wide[head * 2 * WA : (head + 1) * 2 * WA]
            other = pltpu.roll(both, WA, 0)
            upper, lower = (other, both) if level else (both, other)
            both = jnp.where(row < WA, pltpu.roll(upper, WIDE - WA, 1), lower)
            blocks = []
            for pair in range(WO // 2):
                turn = (WO - 2 - 2 * pair) * WA
                block = pltpu.roll(both, (WIDE - turn) % WIDE, 1)[:, :WIN]
                blocks.append(jnp.where(split, -1e30, block))
            block = jnp.transpose(jnp.concatenate(blocks, axis=0))
            bias_ref[level, head * WIN : (head + 1) * WIN, :] = block


def block_kernel(
    core_ref, tokens_ref, cots_ref, below_ref, beside_ref, corner_ref, order_ref,
    wq_ref, wk_ref, wv_ref, proj_ref, up_ref, down_ref, bias_ref,
    result_ref, gtok_ref, mine_ref, other_ref, gbias_ref,
    source_ref, x_ref, cot_ref, bsum_ref, normed_ref, q_ref, k_ref, v_ref, prob_ref, att_ref, res_ref, two_ref, upper_ref, gact_ref, act_ref,
    gup_ref, gres_ref, gmix_ref, gatt_ref, dq_ref, dk_ref, dv_ref, ds_ref, pad_ref, turned_ref,
    unit_ref, inverse_ref, unit_two_ref, inverse_two_ref, mean_ref,
):
    lane = lax.broadcasted_iota(jnp.int32, (1, C), 1) // HEAD
    half_masks = [(lane == head).astype(F32).astype(BF) for head in range(HEADS)]

    def rows_of(part):
        return pl.ds(pl.multiple_of(part * WIN, WIN), WIN)

    near, far = 2 * HALF * 2 * WO, 2 * HALF * 8
    for array, (ref, target) in enumerate(((tokens_ref, x_ref), (cots_ref, cot_ref))):
        for level in range(2):
            for row in range(HALF):
                place = level * HALF + row
                at = place * 2 * WO
                source_ref[at : at + 2 * WO, :] = ref[level, row + HALF].astype(F32)
                source_ref[near + at : near + at + 2 * WO, :] = below_ref[array, level, row].astype(F32)
                at = 2 * near + place * 8
                source_ref[at : at + 8, :] = beside_ref[array, level, row].astype(F32)
                source_ref[far + at : far + at + 8, :] = corner_ref[array, level, row].astype(F32)
        target[...] = dot(order_ref[...], source_ref[...].astype(BF)).astype(BF)

    def first_norm(part, carry):
        rows = rows_of(part)
        mean = row_mean(x_ref[rows, :], exact=True)
        unit, inverse = normal(x_ref[rows, :].astype(F32), mean)
        mean_ref[rows, :] = mean
        unit_ref[rows, :] = unit
        inverse_ref[rows, :] = inverse
        normed_ref[rows, :] = unit.astype(BF)
        return carry

    lax.fori_loop(0, PARTS, first_norm, 0, unroll=4)
    normed = normed_ref[...]
    q_ref[...] = dot(normed, wq_ref[...]).astype(BF)
    k_ref[...] = dot(normed, wk_ref[...]).astype(BF)
    v_ref[...] = dot(normed, wv_ref[...]).astype(BF)

    def attend(part, carry):
        rows = rows_of(part)
        query, key, value = q_ref[rows, :], k_ref[rows, :], v_ref[rows, :]
        level = part % 2
        value_t = jnp.transpose(value)
        chunks = [slice(head * WIN, (head + 1) * WIN) for head in range(HEADS)]
        scores = [dot_rt(key * mask, query) for mask in half_masks]
        for head, chunk in enumerate(chunks):
            score = scores[head] * SCALE + bias_ref[level, chunk, :]
            exponent = jnp.exp(score - jnp.max(score, axis=0, keepdims=True))
            prob = exponent * (1.0 / jnp.sum(exponent, axis=0, keepdims=True))
            prob_ref[part, chunk, :] = prob.astype(BF)
        for head, chunk in enumerate(chunks):
            own = slice(head * HEAD, (head + 1) * HEAD)
            turned_ref[own, :] = dot(value_t[own], prob_ref[part, chunk, :])
        att_ref[rows, :] = jnp.transpose(turned_ref[...]).astype(BF)
        return carry

    lax.fori_loop(0, PARTS, attend, 0, unroll=4)
    res_ref[...] = dot(att_ref[...], proj_ref[...])

    def second_norm(part, carry):
        rows = rows_of(part)
        mixed = res_ref[rows, :].astype(BF)
        residual = x_ref[rows, :].astype(F32) + mixed.astype(F32)
        res_ref[rows, :] = residual
        unit, inverse = normal(residual, mean_ref[rows, :] + row_mean(mixed, exact=True))
        unit_two_ref[rows, :] = unit
        inverse_two_ref[rows, :] = inverse
        two_ref[rows, :] = unit.astype(BF)
        return carry

    lax.fori_loop(0, PARTS, second_norm, 0, unroll=4)
    upper_ref[...] = dot(two_ref[...], up_ref[...])
    gact_ref[...] = dot(cot_ref[...], down_ref[...]).astype(BF)
    step = 32

    def gelu(chunk, carry):
        rows = pl.ds(pl.multiple_of(chunk * step, step), step)
        upper = upper_ref[rows, :]
        cdf = 0.5 + 0.5 * lax.erf(upper * math.sqrt(0.5))
        pdf = jnp.exp(upper * upper * -0.5) * (1.0 / math.sqrt(2.0 * math.pi))
        act_ref[rows, :] = (upper * cdf).astype(BF)
        gup_ref[rows, :] = (gact_ref[rows, :].astype(F32) * (cdf + upper * pdf)).astype(BF)
        return carry

    lax.fori_loop(0, TOKENS // step, gelu, 0)
    result_ref[...] = (res_ref[...] + dot_rt(act_ref[...], down_ref[...])).astype(BF)
    gres_ref[...] = dot_rt(gup_ref[...], up_ref[...])

    def second_back(part, carry):
        rows = rows_of(part)
        unit, inverse = unit_two_ref[rows, :], inverse_two_ref[rows, :]
        grad = gres_ref[rows, :].astype(BF).astype(F32)
        grad = cot_ref[rows, :].astype(F32) + normal_back(unit, inverse, grad)
        gres_ref[rows, :] = grad
        gmix_ref[rows, :] = grad.astype(BF)
        return carry

    lax.fori_loop(0, PARTS, second_back, 0, unroll=4)
    gatt_ref[...] = dot_rt(gmix_ref[...], proj_ref[...]).astype(BF)
    ds_ref[...] = jnp.zeros(ds_ref.shape, F32)
    pad_ref[...] = jnp.zeros(pad_ref.shape, F32)

    def attend_back(part, carry):
        rows = rows_of(part)
        query, key, value = q_ref[rows, :], k_ref[rows, :], v_ref[rows, :]
        gatt = gatt_ref[rows, :]
        level = part % 2
        key_t = jnp.transpose(key)
        chunks = [slice(head * WIN, (head + 1) * WIN) for head in range(HEADS)]
        gowns = [gatt * mask for mask in half_masks]
        gprobs = [dot_rt(value, gown) for gown in gowns]
        gscores = []
        for head, chunk in enumerate(chunks):
            weight = prob_ref[part, chunk, :].astype(F32)
            gscore = weight * (gprobs[head] - jnp.sum(weight * gprobs[head], axis=0, keepdims=True))
            ds_ref[level, chunk, :] += gscore
            gscores.append(gscore.astype(BF))
        gkey = jnp.zeros((WIN, C), F32)
        gvalue = jnp.zeros((WIN, C), F32)
        for head, chunk in enumerate(chunks):
            own = slice(head * HEAD, (head + 1) * HEAD)
            turned_ref[own, :] = dot(key_t[own], gscores[head])
            gkey = gkey + dot(gscores[head], query * half_masks[head])
            gvalue = gvalue + dot(prob_ref[part, chunk, :], gowns[head])
        dq_ref[rows, :] = (jnp.transpose(turned_ref[...]) * SCALE).astype(BF)
        dk_ref[rows, :] = (gkey * SCALE).astype(BF)
        dv_ref[rows, :] = gvalue.astype(BF)
        return carry

    lax.fori_loop(0, PARTS, attend_back, 0, unroll=4)
    normed_grad = dot_rt(dq_ref[...], wq_ref[...])
    normed_grad = normed_grad + dot_rt(dk_ref[...], wk_ref[...])
    res_ref[...] = normed_grad + dot_rt(dv_ref[...], wv_ref[...])

    def first_back(part, carry):
        rows = rows_of(part)
        unit, inverse = unit_ref[rows, :], inverse_ref[rows, :]
        grad = res_ref[rows, :].astype(BF).astype(F32)
        gtok_ref[rows, :] = (gres_ref[rows, :] + normal_back(unit, inverse, grad)).astype(BF)
        return carry

    lax.fori_loop(0, PARTS, first_back, 0, unroll=4)
    first = core_ref[0] == 0

    def put(start, zero, one):
        rows = slice(start, start + zero.shape[0])
        mine_ref[rows, :] = jnp.where(first, zero, one)
        other_ref[rows, :] = jnp.where(first, one, zero).astype(BF)

    gup = dot_lt(two_ref[...], gup_ref[...])
    gdown = dot_lt(cot_ref[...], act_ref[...])
    for chunk in range(6):
        columns = slice(chunk * LANES, (chunk + 1) * LANES)
        put(chunk * C, gup[:, columns], gdown[:, columns])
    normed = normed_ref[...]
    gq = dot_lt(normed, dq_ref[...])
    gk = dot_lt(normed, dk_ref[...])
    gv = dot_lt(normed, dv_ref[...])
    gproj = dot_lt(att_ref[...], gmix_ref[...])
    put(6 * C, gq[:, :LANES], gproj[:, :LANES])
    put(7 * C, gk[:, :LANES], jnp.concatenate([gq[:, LANES:], gk[:, LANES:]], axis=1))
    put(8 * C, gv[:, :LANES], jnp.concatenate([gv[:, LANES:], gproj[:, LANES:]], axis=1))
    mine_ref[9 * C :, :] = jnp.zeros((PACKED - 9 * C, LANES), F32)
    other_ref[9 * C :, :] = jnp.zeros((PACKED - 9 * C, LANES), BF)

    row = lax.broadcasted_iota(jnp.int32, (2 * WA, WIDE), 0)

    def table_grad(level, head):
        place = level * HEADS + head
        pad_ref[place, :, :WIN] = jnp.transpose(ds_ref[level, head * WIN : (head + 1) * WIN, :])
        total = jnp.zeros((2 * WA, WIDE), F32)
        for pair in range(WO // 2):
            turn = (WO - 2 - 2 * pair) * WA
            block = pad_ref[place, pair * 2 * WA : (pair + 1) * 2 * WA, :]
            total = total + (pltpu.roll(block, turn, 1) if turn else block)
        total = jnp.where(row < WA, pltpu.roll(total, WA, 1), total)
        return total + pltpu.roll(total, WA, 0)

    for level in range(2):
        left = jnp.zeros((2 * WA, LANES), F32)
        for pair in range(HEADS // 2):
            both = jnp.where(row < WA, table_grad(level, 2 * pair), table_grad(level, 2 * pair + 1))
            start = pair * 2 * WA
            bsum_ref[level, start : start + 2 * WA, :] = both[:, :LANES]
            bsum_ref[level, MAIN + start : MAIN + start + 2 * WA, :] = both[:, LANES : 2 * LANES]
            rest = both[:, 2 * LANES :]
            left = left + (pltpu.roll(rest, pair * LEFT, 1) if pair else rest)
        bsum_ref[level, 2 * MAIN : 2 * MAIN + 2 * WA, :] = left
        bsum_ref[level, 2 * MAIN + 2 * WA :, :] = jnp.zeros((BIAS_ROWS - 2 * MAIN - 2 * WA, LANES), F32)
    gbias_ref[...] = bsum_ref[...].reshape(2 * BIAS_ROWS, LANES).astype(BF)


def added(one, two):
    return (one.astype(F32) + two.astype(F32)).astype(BF)


def middle_kernel(got_ref, own_ref, came_ref, wait_ref, wide_ref, bias_ref):
    total = jnp.sum(got_ref[...].astype(F32), axis=0).astype(BF)
    for block in range(wide_ref.shape[0]):
        wide_ref[block] = total
    bias_ref[...] = added(own_ref[...], came_ref[...])


def split_kernel(result_ref, gtok_ref, order_ref, own_ref, above_ref, beside_ref, corner_ref):
    near, far = 2 * HALF * 2 * WO, 2 * HALF * 8
    for array, ref in enumerate((result_ref, gtok_ref)):
        rows = dot(order_ref[...], ref[...])
        for level in range(2):
            for row in range(HALF):
                place = level * HALF + row
                at = place * 2 * WO
                own_ref[array, level, row] = rows[at : at + 2 * WO].astype(BF)
                above_ref[array, level, row] = rows[near + at : near + at + 2 * WO].astype(BF)
                at = 2 * near + place * 8
                beside_ref[array, level, row] = rows[at : at + 8].astype(BF)
                corner_ref[array, level, row] = rows[far + at : far + at + 8].astype(BF)


def join_kernel(own_ref, above_ref, beside_ref, corner_ref, result_ref, gtok_ref):
    for array, ref in enumerate((result_ref, gtok_ref)):
        for level in range(2):
            for row in range(HALF):
                for start, long_ref, short_ref in ((0, above_ref, corner_ref), (HALF, own_ref, beside_ref)):
                    rows = long_ref[array, level, row].astype(F32)
                    first = rows[:8] + short_ref[array, level, row].astype(F32)
                    ref[level, start + row] = jnp.concatenate([first, rows[8:]], axis=0).astype(BF)


def final_kernel(
    count, core_ref, mine_ref, other_ref, gbias_ref, back_ref,
    qkv_ref, proj_ref, up_ref, down_ref, bias_ref,
):
    first = core_ref[0] == 0
    mine = mine_ref[...].astype(F32)[: 9 * C]
    other = other_ref[...].astype(F32)[: 9 * C]
    total = jnp.sum(mine * mine) + jnp.sum(other * other)
    factor = jnp.minimum(1.0, math.sqrt(count) / (jnp.sqrt(jnp.full((8, LANES), total)) + 1e-06))[:1]
    zero = jnp.where(first, mine, other) * factor
    one = jnp.where(first, other, mine) * factor

    def chunk(half, place):
        return half[place * C : (place + 1) * C]

    for place in range(6):
        up_ref[:, place * LANES : (place + 1) * LANES] = chunk(zero, place)
        down_ref[:, place * LANES : (place + 1) * LANES] = chunk(one, place)
    last = C - LANES
    left, right = chunk(one, 7), chunk(one, 8)
    qkv_ref[:, :C] = jnp.concatenate([chunk(zero, 6), left[:, :last]], axis=1)
    qkv_ref[:, C : 2 * C] = jnp.concatenate([chunk(zero, 7), left[:, last:]], axis=1)
    qkv_ref[:, 2 * C :] = jnp.concatenate([chunk(zero, 8), right[:, :last]], axis=1)
    proj_ref[...] = jnp.concatenate([chunk(one, 6), right[:, last:]], axis=1)

    sums = gbias_ref[...].astype(F32)
    tables = []
    for level in range(2):
        packed = sums[level * BIAS_ROWS : (level + 1) * BIAS_ROWS]
        left = packed[2 * MAIN : 2 * MAIN + 2 * WA]
        left = [left] + [pltpu.roll(left, LANES - pair * LEFT, 1) for pair in range(1, HEADS // 2)]
        rows = [packed[:MAIN], packed[MAIN : 2 * MAIN], jnp.concatenate(left, axis=0)]
        rows = jnp.concatenate(rows, axis=1).astype(BF)
        tables.append(dot(rows, back_ref[level]) * factor[:, :1])
    row = lax.broadcasted_iota(jnp.int32, (2 * WA, 2 * CUT), 0)
    for pair in range(HEADS // 2):
        upper, lower = [table[pair * 2 * WA : (pair + 1) * 2 * WA] for table in tables]
        bias_ref[0, 0, 2 * pair] = jnp.where(row < WA, upper, pltpu.roll(lower, WA, 0))
        bias_ref[0, 0, 2 * pair + 1] = jnp.where(row < WA, pltpu.roll(upper, WA, 0), lower)


def call(kernel, outs, scalars, arrays, scratch=(), limit=SMALL):
    spaces = [pl.BlockSpec(memory_space=pltpu.SMEM)] * scalars
    spaces += [pl.BlockSpec(memory_space=pltpu.VMEM)] * arrays
    return pl.pallas_call(
        kernel,
        out_shape=outs,
        in_specs=spaces,
        out_specs=[pl.BlockSpec(memory_space=pltpu.VMEM)] * len(outs),
        scratch_shapes=scratch,
        compiler_params=pltpu.CompilerParams(vmem_limit_bytes=limit),
    )


def shape(*sizes, kind=F32):
    return jax.ShapeDtypeStruct(sizes, kind)


def from_next(block, axes, distance):
    sizes = [lax.axis_size(axis) for axis in axes]
    route = []
    for place in np.ndindex(*sizes):
        source = [(i + distance) % size for i, size in zip(place, sizes)]
        route.append((int(np.ravel_multi_index(source, sizes)), int(np.ravel_multi_index(place, sizes))))
    return lax.ppermute(block, tuple(axes), route)


def roll_back_start(result, grad_tokens):
    wide, narrow = shape(2, 2, HALF, 2 * WO, C, kind=BF), shape(2, 2, HALF, 8, C, kind=BF)
    order = jnp.asarray(window_order().T, BF)
    pieces = call(split_kernel, [wide, wide, narrow, narrow], 0, 3)(result, grad_tokens, order)
    own, above, beside, corner = pieces
    above = from_next(above, ["lat"], -1)
    corner = from_next(corner, ["lat", "lon"], -1)
    beside = from_next(beside, ["lon"], -1)
    return own, above, beside, corner


def roll_back_end(pieces):
    whole = shape(2, WA, 2 * WO, C, kind=BF)
    return call(join_kernel, [whole, whole], 0, 4)(*pieces)


def gradient_sums(mine, other, bias, pieces):
    lat, lon = lax.axis_size("lat"), lax.axis_size("lon")
    half, depth = lat // 2, lon // 2
    pairs = [(i, i ^ 1) for i in range(lat)]
    planes = [
        [(2 * i + core) * lon + 2 * z + low for i in range(half) for low in range(2)]
        for core in range(2)
        for z in range(depth)
    ]
    columns = [[2 * z + low for z in range(depth)] for low in range(2)]
    share = PACKED // lat

    def partner(block, distance):
        return lax.ppermute(block, "lon", [(i, i ^ distance) for i in range(lon)])

    def middle(got, own, came, blocks, wait):
        outs = [shape(blocks, share, LANES, kind=BF), shape(2 * BIAS_ROWS, LANES, kind=BF)]
        return call(middle_kernel, outs, 0, 4)(got, own, came, wait)

    mine = mine + lax.ppermute(other, "lat", pairs).astype(F32)
    mine = mine.astype(BF).reshape(lat, share, LANES)
    got = lax.all_to_all(mine, ("lat", "lon"), 0, 0, axis_index_groups=planes)
    bias = added(bias, partner(bias, 1))
    wide, bias = middle(got, bias, partner(bias, 2), depth, bias[:8])
    got = lax.all_to_all(wide, "lon", 0, 0, axis_index_groups=columns)
    wait = functools.reduce(added, [piece[0, 0, 0, :8] for piece in pieces[1:]])
    wide, bias = middle(got, bias, partner(bias, 4), lat, wait)
    bias = added(bias, partner(bias, 8))
    mine = lax.all_to_all(wide, ("lat", "lon"), 0, 0, axis_index_groups=planes)
    mine = lax.dynamic_update_slice(mine, bias[None, :16], (lat - 1, share - 16, 0))
    other = lax.ppermute(mine, "lat", pairs)
    return mine.reshape(PACKED, LANES), other.reshape(PACKED, LANES), bias


def on_device(tokens, w_qkv, w_proj, w_up, w_down, earth_bias, cotangent):
    band = lax.axis_index("lat")
    bands = lax.axis_size("lat")
    core = (band % 2).astype(jnp.int32).reshape(1)
    last = (band == bands - 1).astype(jnp.int32).reshape(1)

    wide, narrow = shape(2, 2, HALF, 2 * WO, C, kind=BF), shape(2, 2, HALF, 8, C, kind=BF)
    below, beside, corner = call(halo_kernel, [wide, narrow, narrow], 0, 2)(tokens, cotangent)
    below = from_next(below, ["lat"], 1)
    corner = from_next(corner, ["lat", "lon"], 1)
    beside = from_next(beside, ["lon"], 1)
    back = table_back()
    order = jnp.asarray(back.transpose(0, 2, 1), BF)
    bias = call(bias_kernel, [shape(2, HEADS * WIN, WIN)], 1, 2)(last, earth_bias, order)[0]

    def tokens_of(width, kind=BF):
        return pltpu.VMEM((TOKENS, width), kind)

    outs = [
        shape(TOKENS, C, kind=BF),
        shape(TOKENS, C, kind=BF),
        shape(PACKED, LANES),
        shape(PACKED, LANES, kind=BF),
        shape(2 * BIAS_ROWS, LANES, kind=BF),
    ]
    scratch = [pltpu.VMEM((SOURCES, C), F32), tokens_of(C), tokens_of(C), pltpu.VMEM((2, BIAS_ROWS, LANES), F32)]
    scratch += [tokens_of(C)] * 4 + [pltpu.VMEM((PARTS, HEADS * WIN, WIN), BF), tokens_of(C), tokens_of(C, F32)]
    scratch += [tokens_of(C), tokens_of(HID, F32)] + [tokens_of(HID)] * 3 + [tokens_of(C, F32)]
    scratch += [tokens_of(C)] * 5 + [pltpu.VMEM((2, HEADS * WIN, WIN), F32)]
    scratch += [pltpu.VMEM((2 * HEADS, WIN, WIDE), F32), pltpu.VMEM((C, WIN), F32)]
    scratch += [tokens_of(C, F32)] * 5
    result, grad_tokens, *grads = call(block_kernel, outs, 1, 13, scratch, limit=LARGE)(
        core, tokens, cotangent, below, beside, corner, jnp.asarray(window_order(), BF),
        w_qkv[:, :C], w_qkv[:, C : 2 * C], w_qkv[:, 2 * C :], w_proj, w_up, w_down.T, bias,
    )
    pieces = roll_back_start(result, grad_tokens)
    sums = gradient_sums(*grads, pieces)
    result, grad_tokens = roll_back_end(pieces)

    count = w_qkv.size + w_proj.size + w_up.size + w_down.size + earth_bias.size * bands
    outs = [shape(C, 3 * C), shape(C, C), shape(C, HID), shape(C, HID), shape(1, 1, HEADS, 2 * WA, 2 * CUT)]
    grads = call(functools.partial(final_kernel, count), outs, 1, 4)(core, *sums, jnp.asarray(back, BF))
    return (result, grad_tokens, *grads[:3], grads[3].T, grads[4])


def solution(mesh):
    placed = (
        P(None, "lat", "lon", None),
        P(),
        P(),
        P(),
        P(),
        P("lat", None, None, None, None),
        P(None, "lat", "lon", None),
    )
    return jax.shard_map(
        on_device,
        mesh=mesh,
        in_specs=placed,
        out_specs=(
            P(None, "lat", "lon", None),
            P(None, "lat", "lon", None),
            P(),
            P(),
            P(),
            P(),
            P("lat", None, None, None, None),
        ),
        check_vma=False,
    )
```

```python
import functools
import math

import jax
import jax.numpy as jnp
import numpy as np
from jax import lax
from jax.experimental import pallas as pl
from jax.experimental.pallas import tpu as pltpu
from jax.sharding import PartitionSpec as P

WA = 12
WO = 12
HALF = 6
HEADS = 6
HEAD = 32
WIN = WA * WO
SPAN = 2 * WO - 1
CUT = WA * SPAN
WIDE = 384
LANES = 128
C = 192
HID = 768
TOKENS = 576
PARTS = 4
PACKED = 1792
SOURCES = 768
MAIN = HEADS * WA
BIAS_ROWS = 176
LEFT = CUT - 2 * LANES
EPS = 1e-05
SCALE = HEAD ** (-0.5)
LARGE = 28 * 1024 * 1024
SMALL = 12 * 1024 * 1024
BF = jnp.bfloat16
F32 = jnp.float32


def table_order():
    lane = np.arange(CUT)
    order = np.zeros((CUT, WIDE), np.float32)
    order[(lane % WA) * SPAN + SPAN - 1 - lane // WA, lane] = 1.0
    return order


def table_back():
    back = np.zeros((2, WIDE, 2 * CUT), np.float32)
    for level in range(2):
        back[level, :, level * CUT : (level + 1) * CUT] = table_order().T
    return back


def window_order():
    order = np.zeros((TOKENS, SOURCES), np.float32)
    near, far = 2 * HALF * 2 * WO, 2 * HALF * 8
    for window, level, column, row in np.ndindex(2, 2, WO, WA):
        token = ((window * 2 + level) * WO + column) * WA + row
        place, across = (1 - level) * HALF + row % HALF, window * WO + column + HALF
        inside = across < 2 * WO
        at = place * 2 * WO + across if inside else 2 * near + place * 8 + across - 2 * WO
        if row >= HALF:
            at += near if inside else far
        order[token, at] = 1.0
    return order


def dot(a, b):
    return jnp.dot(a, b, preferred_element_type=F32)


def dot_rt(a, b):
    return lax.dot_general(a, b, (((1,), (1,)), ((), ())), preferred_element_type=F32)


def dot_lt(a, b):
    return lax.dot_general(a, b, (((0,), (0,)), ((), ())), preferred_element_type=F32)


def row_mean(values, exact=False):
    ones = jnp.full((C, C), 1.0, BF)
    high = values.astype(BF)
    total = dot(high, ones)
    if not exact:
        total = total + dot((values - high.astype(F32)).astype(BF), ones)
    return total * (1.0 / C)


def normal(values, mean):
    centred = values - mean
    inverse = lax.rsqrt(row_mean(centred * centred) + EPS)
    return centred * inverse, inverse


def normal_back(unit, inverse, grad):
    first = row_mean(grad, exact=True)
    second = row_mean(grad * unit)
    return inverse * (grad - first - unit * second)


def halo_kernel(tokens_ref, cot_ref, below_ref, beside_ref, corner_ref):
    for array, ref in enumerate((tokens_ref, cot_ref)):
        for level in range(2):
            for row in range(HALF):
                below_ref[array, level, row] = ref[level, row]
                beside_ref[array, level, row] = ref[level, row + HALF].astype(F32)[:8].astype(BF)
                corner_ref[array, level, row] = ref[level, row].astype(F32)[:8].astype(BF)


def bias_kernel(last_ref, table_ref, order_ref, bias_ref):
    table = table_ref[0, 0].reshape(HEADS * 2 * WA, 2 * CUT)
    high = table.astype(BF)
    rest = table - high.astype(F32)
    middle = rest.astype(BF)
    low = (rest - middle.astype(F32)).astype(BF)
    row = lax.broadcasted_iota(jnp.int32, (2 * WA, WIDE), 0)
    row_i = lax.broadcasted_iota(jnp.int32, (2 * WA, WIN), 0) % WA
    row_j = lax.broadcasted_iota(jnp.int32, (2 * WA, WIN), 1) % WA
    split = (row_i >= HALF) != (row_j >= HALF)
    split = jnp.logical_and(split, last_ref[0] == 1)
    for level in range(2):
        own = slice(level * CUT, (level + 1) * CUT)
        wide = sum(dot(term[:, own], order_ref[...]) for term in (low, middle, high))
        for head in range(HEADS):
            both = wide[head * 2 * WA : (head + 1) * 2 * WA]
            other = pltpu.roll(both, WA, 0)
            upper, lower = (other, both) if level else (both, other)
            both = jnp.where(row < WA, pltpu.roll(upper, WIDE - WA, 1), lower)
            blocks = []
            for pair in range(WO // 2):
                turn = (WO - 2 - 2 * pair) * WA
                block = pltpu.roll(both, (WIDE - turn) % WIDE, 1)[:, :WIN]
                blocks.append(jnp.where(split, -1e30, block))
            block = jnp.transpose(jnp.concatenate(blocks, axis=0))
            bias_ref[level, head * WIN : (head + 1) * WIN, :] = block


def block_kernel(
    core_ref, tokens_ref, cots_ref, below_ref, beside_ref, corner_ref, order_ref,
    qkv_ref, proj_ref, up_ref, down_ref, bias_ref,
    result_ref, gtok_ref, mine_ref, other_ref, gbias_ref,
    source_ref, x_ref, cot_ref, bsum_ref, normed_ref, q_ref, k_ref, v_ref, prob_ref, att_ref, res_ref, two_ref, upper_ref, gact_ref, act_ref,
    gup_ref, gres_ref, gmix_ref, gatt_ref, dq_ref, dk_ref, dv_ref, ds_ref, pad_ref, turned_ref,
    unit_ref, inverse_ref, unit_two_ref, inverse_two_ref, mean_ref,
):
    lane = lax.broadcasted_iota(jnp.int32, (1, C), 1) // HEAD
    half_masks = [(lane == head).astype(F32).astype(BF) for head in range(HEADS)]

    def rows_of(part):
        return pl.ds(pl.multiple_of(part * WIN, WIN), WIN)

    near, far = 2 * HALF * 2 * WO, 2 * HALF * 8
    for array, (ref, target) in enumerate(((tokens_ref, x_ref), (cots_ref, cot_ref))):
        for level in range(2):
            for row in range(HALF):
                place = level * HALF + row
                at = place * 2 * WO
                source_ref[at : at + 2 * WO, :] = ref[level, row + HALF].astype(F32)
                source_ref[near + at : near + at + 2 * WO, :] = below_ref[array, level, row].astype(F32)
                at = 2 * near + place * 8
                source_ref[at : at + 8, :] = beside_ref[array, level, row].astype(F32)
                source_ref[far + at : far + at + 8, :] = corner_ref[array, level, row].astype(F32)
        target[...] = dot(order_ref[...], source_ref[...].astype(BF)).astype(BF)

    def first_norm(part, carry):
        rows = rows_of(part)
        mean = row_mean(x_ref[rows, :], exact=True)
        unit, inverse = normal(x_ref[rows, :].astype(F32), mean)
        mean_ref[rows, :] = mean
        unit_ref[rows, :] = unit
        inverse_ref[rows, :] = inverse
        normed_ref[rows, :] = unit.astype(BF)
        return carry

    lax.fori_loop(0, PARTS, first_norm, 0, unroll=4)
    normed = normed_ref[...]
    weights = [qkv_ref[:, part * C : (part + 1) * C] for part in range(3)]
    for target, weight in zip((q_ref, k_ref, v_ref), weights):
        target[...] = dot(normed, weight).astype(BF)

    def attend(part, carry):
        rows = rows_of(part)
        query, key, value = q_ref[rows, :], k_ref[rows, :], v_ref[rows, :]
        level = part % 2
        value_t = jnp.transpose(value)
        chunks = [slice(head * WIN, (head + 1) * WIN) for head in range(HEADS)]
        scores = [dot_rt(key * mask, query) for mask in half_masks]
        for head, chunk in enumerate(chunks):
            score = scores[head] * SCALE + bias_ref[level, chunk, :]
            exponent = jnp.exp(score - jnp.max(score, axis=0, keepdims=True))
            prob = exponent * (1.0 / jnp.sum(exponent, axis=0, keepdims=True))
            prob_ref[part, chunk, :] = prob.astype(BF)
        for head, chunk in enumerate(chunks):
            own = slice(head * HEAD, (head + 1) * HEAD)
            turned_ref[own, :] = dot(value_t[own], prob_ref[part, chunk, :])
        att_ref[rows, :] = jnp.transpose(turned_ref[...]).astype(BF)
        return carry

    lax.fori_loop(0, PARTS, attend, 0, unroll=4)
    res_ref[...] = dot(att_ref[...], proj_ref[...])

    def second_norm(part, carry):
        rows = rows_of(part)
        mixed = res_ref[rows, :].astype(BF)
        residual = x_ref[rows, :].astype(F32) + mixed.astype(F32)
        res_ref[rows, :] = residual
        unit, inverse = normal(residual, mean_ref[rows, :] + row_mean(mixed, exact=True))
        unit_two_ref[rows, :] = unit
        inverse_two_ref[rows, :] = inverse
        two_ref[rows, :] = unit.astype(BF)
        return carry

    lax.fori_loop(0, PARTS, second_norm, 0, unroll=4)
    upper_ref[...] = dot(two_ref[...], up_ref[...])
    gact_ref[...] = dot(cot_ref[...], down_ref[...]).astype(BF)
    step = 32

    def gelu(chunk, carry):
        rows = pl.ds(pl.multiple_of(chunk * step, step), step)
        upper = upper_ref[rows, :]
        cdf = 0.5 + 0.5 * lax.erf(upper * math.sqrt(0.5))
        pdf = jnp.exp(upper * upper * -0.5) * (1.0 / math.sqrt(2.0 * math.pi))
        act_ref[rows, :] = (upper * cdf).astype(BF)
        gup_ref[rows, :] = (gact_ref[rows, :].astype(F32) * (cdf + upper * pdf)).astype(BF)
        return carry

    lax.fori_loop(0, TOKENS // step, gelu, 0)
    result_ref[...] = (res_ref[...] + dot_rt(act_ref[...], down_ref[...])).astype(BF)
    gres_ref[...] = dot_rt(gup_ref[...], up_ref[...])

    def second_back(part, carry):
        rows = rows_of(part)
        unit, inverse = unit_two_ref[rows, :], inverse_two_ref[rows, :]
        grad = gres_ref[rows, :].astype(BF).astype(F32)
        grad = cot_ref[rows, :].astype(F32) + normal_back(unit, inverse, grad)
        gres_ref[rows, :] = grad
        gmix_ref[rows, :] = grad.astype(BF)
        return carry

    lax.fori_loop(0, PARTS, second_back, 0, unroll=4)
    gatt_ref[...] = dot_rt(gmix_ref[...], proj_ref[...]).astype(BF)
    ds_ref[...] = jnp.zeros(ds_ref.shape, F32)
    pad_ref[...] = jnp.zeros(pad_ref.shape, F32)

    def attend_back(part, carry):
        rows = rows_of(part)
        query, key, value = q_ref[rows, :], k_ref[rows, :], v_ref[rows, :]
        gatt = gatt_ref[rows, :]
        level = part % 2
        key_t = jnp.transpose(key)
        chunks = [slice(head * WIN, (head + 1) * WIN) for head in range(HEADS)]
        gowns = [gatt * mask for mask in half_masks]
        gprobs = [dot_rt(value, gown) for gown in gowns]
        gscores = []
        for head, chunk in enumerate(chunks):
            weight = prob_ref[part, chunk, :].astype(F32)
            gscore = weight * (gprobs[head] - jnp.sum(weight * gprobs[head], axis=0, keepdims=True))
            ds_ref[level, chunk, :] += gscore
            gscores.append(gscore.astype(BF))
        gkey = jnp.zeros((WIN, C), F32)
        gvalue = jnp.zeros((WIN, C), F32)
        for head, chunk in enumerate(chunks):
            own = slice(head * HEAD, (head + 1) * HEAD)
            turned_ref[own, :] = dot(key_t[own], gscores[head])
            gkey = gkey + dot(gscores[head], query * half_masks[head])
            gvalue = gvalue + dot(prob_ref[part, chunk, :], gowns[head])
        dq_ref[rows, :] = (jnp.transpose(turned_ref[...]) * SCALE).astype(BF)
        dk_ref[rows, :] = (gkey * SCALE).astype(BF)
        dv_ref[rows, :] = gvalue.astype(BF)
        return carry

    lax.fori_loop(0, PARTS, attend_back, 0, unroll=4)
    res_ref[...] = sum(dot_rt(ref[...], weight) for ref, weight in zip((dq_ref, dk_ref, dv_ref), weights))

    def first_back(part, carry):
        rows = rows_of(part)
        unit, inverse = unit_ref[rows, :], inverse_ref[rows, :]
        grad = res_ref[rows, :].astype(BF).astype(F32)
        gtok_ref[rows, :] = (gres_ref[rows, :] + normal_back(unit, inverse, grad)).astype(BF)
        return carry

    lax.fori_loop(0, PARTS, first_back, 0, unroll=4)
    first = core_ref[0] == 0

    def put(start, zero, one):
        rows = slice(start, start + zero.shape[0])
        mine_ref[rows, :] = jnp.where(first, zero, one)
        other_ref[rows, :] = jnp.where(first, one, zero).astype(BF)

    gup = dot_lt(two_ref[...], gup_ref[...])
    gdown = dot_lt(cot_ref[...], act_ref[...])
    for chunk in range(6):
        columns = slice(chunk * LANES, (chunk + 1) * LANES)
        put(chunk * C, gup[:, columns], gdown[:, columns])
    normed = normed_ref[...]
    gq = dot_lt(normed, dq_ref[...])
    gk = dot_lt(normed, dk_ref[...])
    gv = dot_lt(normed, dv_ref[...])
    gproj = dot_lt(att_ref[...], gmix_ref[...])
    put(6 * C, gq[:, :LANES], gproj[:, :LANES])
    put(7 * C, gk[:, :LANES], jnp.concatenate([gq[:, LANES:], gk[:, LANES:]], axis=1))
    put(8 * C, gv[:, :LANES], jnp.concatenate([gv[:, LANES:], gproj[:, LANES:]], axis=1))
    mine_ref[9 * C :, :] = jnp.zeros((PACKED - 9 * C, LANES), F32)
    other_ref[9 * C :, :] = jnp.zeros((PACKED - 9 * C, LANES), BF)

    row = lax.broadcasted_iota(jnp.int32, (2 * WA, WIDE), 0)

    def table_grad(level, head):
        place = level * HEADS + head
        pad_ref[place, :, :WIN] = jnp.transpose(ds_ref[level, head * WIN : (head + 1) * WIN, :])
        total = jnp.zeros((2 * WA, WIDE), F32)
        for pair in range(WO // 2):
            turn = (WO - 2 - 2 * pair) * WA
            block = pad_ref[place, pair * 2 * WA : (pair + 1) * 2 * WA, :]
            total = total + (pltpu.roll(block, turn, 1) if turn else block)
        total = jnp.where(row < WA, pltpu.roll(total, WA, 1), total)
        return total + pltpu.roll(total, WA, 0)

    for level in range(2):
        left = jnp.zeros((2 * WA, LANES), F32)
        for pair in range(HEADS // 2):
            both = jnp.where(row < WA, table_grad(level, 2 * pair), table_grad(level, 2 * pair + 1))
            start = pair * 2 * WA
            bsum_ref[level, start : start + 2 * WA, :] = both[:, :LANES]
            bsum_ref[level, MAIN + start : MAIN + start + 2 * WA, :] = both[:, LANES : 2 * LANES]
            rest = both[:, 2 * LANES :]
            left = left + (pltpu.roll(rest, pair * LEFT, 1) if pair else rest)
        bsum_ref[level, 2 * MAIN : 2 * MAIN + 2 * WA, :] = left
        bsum_ref[level, 2 * MAIN + 2 * WA :, :] = jnp.zeros((BIAS_ROWS - 2 * MAIN - 2 * WA, LANES), F32)
    gbias_ref[...] = bsum_ref[...].reshape(2 * BIAS_ROWS, LANES).astype(BF)


def added(one, two):
    return (one.astype(F32) + two.astype(F32)).astype(BF)


def first_kernel(mine_ref, got_ref, own_ref, came_ref, sum_ref, bias_ref):
    sum_ref[...] = (mine_ref[...] + got_ref[...].astype(F32)).astype(BF)
    bias_ref[...] = added(own_ref[...], came_ref[...])


def middle_kernel(got_ref, own_ref, came_ref, wait_ref, wide_ref, bias_ref):
    total = jnp.sum(got_ref[...].astype(F32), axis=0).astype(BF)
    for block in range(wide_ref.shape[0]):
        wide_ref[block] = total
    bias_ref[...] = added(own_ref[...], came_ref[...])


def split_kernel(result_ref, gtok_ref, order_ref, own_ref, above_ref, beside_ref, corner_ref):
    near, far = 2 * HALF * 2 * WO, 2 * HALF * 8
    for array, ref in enumerate((result_ref, gtok_ref)):
        rows = dot(order_ref[...], ref[...])
        for level in range(2):
            for row in range(HALF):
                place = level * HALF + row
                at = place * 2 * WO
                own_ref[array, level, row] = rows[at : at + 2 * WO].astype(BF)
                above_ref[array, level, row] = rows[near + at : near + at + 2 * WO].astype(BF)
                at = 2 * near + place * 8
                beside_ref[array, level, row] = rows[at : at + 8].astype(BF)
                corner_ref[array, level, row] = rows[far + at : far + at + 8].astype(BF)


def join_kernel(own_ref, above_ref, beside_ref, corner_ref, result_ref, gtok_ref):
    for array, ref in enumerate((result_ref, gtok_ref)):
        for level in range(2):
            for row in range(HALF):
                for start, long_ref, short_ref in ((0, above_ref, corner_ref), (HALF, own_ref, beside_ref)):
                    rows = long_ref[array, level, row].astype(F32)
                    first = rows[:8] + short_ref[array, level, row].astype(F32)
                    ref[level, start + row] = jnp.concatenate([first, rows[8:]], axis=0).astype(BF)


def final_kernel(
    count, core_ref, mine_ref, other_ref, gbias_ref, back_ref,
    qkv_ref, proj_ref, up_ref, down_ref, bias_ref,
):
    first = core_ref[0] == 0
    mine = mine_ref[...].astype(F32)[: 9 * C]
    other = other_ref[...].astype(F32)[: 9 * C]
    total = jnp.sum(mine * mine) + jnp.sum(other * other)
    factor = jnp.minimum(1.0, math.sqrt(count) / (jnp.sqrt(jnp.full((8, LANES), total)) + 1e-06))[:1]
    zero = jnp.where(first, mine, other) * factor
    one = jnp.where(first, other, mine) * factor

    def chunk(half, place):
        return half[place * C : (place + 1) * C]

    for place in range(6):
        up_ref[:, place * LANES : (place + 1) * LANES] = chunk(zero, place)
        down_ref[:, place * LANES : (place + 1) * LANES] = chunk(one, place)
    last = C - LANES
    left, right = chunk(one, 7), chunk(one, 8)
    qkv_ref[:, :C] = jnp.concatenate([chunk(zero, 6), left[:, :last]], axis=1)
    qkv_ref[:, C : 2 * C] = jnp.concatenate([chunk(zero, 7), left[:, last:]], axis=1)
    qkv_ref[:, 2 * C :] = jnp.concatenate([chunk(zero, 8), right[:, :last]], axis=1)
    proj_ref[...] = jnp.concatenate([chunk(one, 6), right[:, last:]], axis=1)

    sums = gbias_ref[...].astype(F32)
    tables = []
    for level in range(2):
        packed = sums[level * BIAS_ROWS : (level + 1) * BIAS_ROWS]
        left = packed[2 * MAIN : 2 * MAIN + 2 * WA]
        left = [left] + [pltpu.roll(left, LANES - pair * LEFT, 1) for pair in range(1, HEADS // 2)]
        rows = [packed[:MAIN], packed[MAIN : 2 * MAIN], jnp.concatenate(left, axis=0)]
        rows = jnp.concatenate(rows, axis=1).astype(BF)
        tables.append(dot(rows, back_ref[level]) * factor[:, :1])
    row = lax.broadcasted_iota(jnp.int32, (2 * WA, 2 * CUT), 0)
    for pair in range(HEADS // 2):
        upper, lower = [table[pair * 2 * WA : (pair + 1) * 2 * WA] for table in tables]
        bias_ref[0, 0, 2 * pair] = jnp.where(row < WA, upper, pltpu.roll(lower, WA, 0))
        bias_ref[0, 0, 2 * pair + 1] = jnp.where(row < WA, pltpu.roll(upper, WA, 0), lower)


def call(kernel, outs, scalars, arrays, scratch=(), limit=SMALL):
    spaces = [pl.BlockSpec(memory_space=pltpu.SMEM)] * scalars
    spaces += [pl.BlockSpec(memory_space=pltpu.VMEM)] * arrays
    return pl.pallas_call(
        kernel,
        out_shape=outs,
        in_specs=spaces,
        out_specs=[pl.BlockSpec(memory_space=pltpu.VMEM)] * len(outs),
        scratch_shapes=scratch,
        compiler_params=pltpu.CompilerParams(vmem_limit_bytes=limit),
    )


def shape(*sizes, kind=F32):
    return jax.ShapeDtypeStruct(sizes, kind)


def from_next(block, axes, distance):
    sizes = [lax.axis_size(axis) for axis in axes]
    route = []
    for place in np.ndindex(*sizes):
        source = [(i + distance) % size for i, size in zip(place, sizes)]
        route.append((int(np.ravel_multi_index(source, sizes)), int(np.ravel_multi_index(place, sizes))))
    return lax.ppermute(block, tuple(axes), route)


def roll_back_start(result, grad_tokens):
    wide, narrow = shape(2, 2, HALF, 2 * WO, C, kind=BF), shape(2, 2, HALF, 8, C, kind=BF)
    order = jnp.asarray(window_order().T, BF)
    pieces = call(split_kernel, [wide, wide, narrow, narrow], 0, 3)(result, grad_tokens, order)
    own, above, beside, corner = pieces
    above = from_next(above, ["lat"], -1)
    corner = from_next(corner, ["lat", "lon"], -1)
    beside = from_next(beside, ["lon"], -1)
    return own, above, beside, corner


def roll_back_end(pieces):
    whole = shape(2, WA, 2 * WO, C, kind=BF)
    return call(join_kernel, [whole, whole], 0, 4)(*pieces)


def gradient_sums(mine, other, bias, pieces):
    lat, lon = lax.axis_size("lat"), lax.axis_size("lon")
    half, depth = lat // 2, lon // 2
    pairs = [(i, i ^ 1) for i in range(lat)]
    planes = [
        [(2 * i + core) * lon + 2 * z + low for i in range(half) for low in range(2)]
        for core in range(2)
        for z in range(depth)
    ]
    columns = [[2 * z + low for z in range(depth)] for low in range(2)]
    share = PACKED // lat

    def partner(block, distance):
        return lax.ppermute(block, "lon", [(i, i ^ distance) for i in range(lon)])

    def middle(got, own, came, blocks, wait):
        outs = [shape(blocks, share, LANES, kind=BF), shape(2 * BIAS_ROWS, LANES, kind=BF)]
        return call(middle_kernel, outs, 0, 4)(got, own, came, wait)

    own, above, beside, corner = pieces
    outs = [shape(PACKED, LANES, kind=BF), shape(2 * BIAS_ROWS, LANES, kind=BF)]
    mine, bias = call(first_kernel, outs, 0, 4)(mine, lax.ppermute(other, "lat", pairs), bias, partner(bias, 1))
    got = lax.all_to_all(mine.reshape(lat, share, LANES), ("lat", "lon"), 0, 0, axis_index_groups=planes)
    wide, bias = middle(got, bias, partner(bias, 2), depth, beside[0, 0, 0])
    got = lax.all_to_all(wide, "lon", 0, 0, axis_index_groups=columns)
    wide, bias = middle(got, bias, partner(bias, 4), lat, above[0, 0, 0, :8])
    bias = added(bias, partner(bias, 8))
    mine = lax.all_to_all(wide, ("lat", "lon"), 0, 0, axis_index_groups=planes)
    wait = added(bias[:8], corner[0, 0, 0, :, :LANES])
    mine = lax.dynamic_update_slice(mine, wait[None], (lat - 1, share - 8, 0))
    other = lax.ppermute(mine, "lat", pairs)
    return mine.reshape(PACKED, LANES), other.reshape(PACKED, LANES), bias


def on_device(tokens, w_qkv, w_proj, w_up, w_down, earth_bias, cotangent):
    band = lax.axis_index("lat")
    bands = lax.axis_size("lat")
    core = (band % 2).astype(jnp.int32).reshape(1)
    last = (band == bands - 1).astype(jnp.int32).reshape(1)

    wide, narrow = shape(2, 2, HALF, 2 * WO, C, kind=BF), shape(2, 2, HALF, 8, C, kind=BF)
    below, beside, corner = call(halo_kernel, [wide, narrow, narrow], 0, 2)(tokens, cotangent)
    below = from_next(below, ["lat"], 1)
    corner = from_next(corner, ["lat", "lon"], 1)
    beside = from_next(beside, ["lon"], 1)
    back = table_back()
    order = jnp.asarray(table_order(), BF)
    bias = call(bias_kernel, [shape(2, HEADS * WIN, WIN)], 1, 2)(last, earth_bias, order)[0]

    def tokens_of(width, kind=BF):
        return pltpu.VMEM((TOKENS, width), kind)

    outs = [
        shape(TOKENS, C, kind=BF),
        shape(TOKENS, C, kind=BF),
        shape(PACKED, LANES),
        shape(PACKED, LANES, kind=BF),
        shape(2 * BIAS_ROWS, LANES, kind=BF),
    ]
    scratch = [pltpu.VMEM((SOURCES, C), F32), tokens_of(C), tokens_of(C), pltpu.VMEM((2, BIAS_ROWS, LANES), F32)]
    scratch += [tokens_of(C)] * 4 + [pltpu.VMEM((PARTS, HEADS * WIN, WIN), BF), tokens_of(C), tokens_of(C, F32)]
    scratch += [tokens_of(C), tokens_of(HID, F32)] + [tokens_of(HID)] * 3 + [tokens_of(C, F32)]
    scratch += [tokens_of(C)] * 5 + [pltpu.VMEM((2, HEADS * WIN, WIN), F32)]
    scratch += [pltpu.VMEM((2 * HEADS, WIN, WIDE), F32), pltpu.VMEM((C, WIN), F32)]
    scratch += [tokens_of(C, F32)] * 5
    result, grad_tokens, *grads = call(block_kernel, outs, 1, 11, scratch, limit=LARGE)(
        core, tokens, cotangent, below, beside, corner, jnp.asarray(window_order(), BF),
        w_qkv, w_proj, w_up, w_down.T, bias,
    )
    pieces = roll_back_start(result, grad_tokens)
    sums = gradient_sums(*grads, pieces)
    result, grad_tokens = roll_back_end(pieces)

    count = w_qkv.size + w_proj.size + w_up.size + w_down.size + earth_bias.size * bands
    outs = [shape(C, 3 * C), shape(C, C), shape(C, HID), shape(C, HID), shape(1, 1, HEADS, 2 * WA, 2 * CUT)]
    grads = call(functools.partial(final_kernel, count), outs, 1, 4)(core, *sums, jnp.asarray(back, BF))
    return (result, grad_tokens, *grads[:3], grads[3].T, grads[4])


def solution(mesh):
    placed = (
        P(None, "lat", "lon", None),
        P(),
        P(),
        P(),
        P(),
        P("lat", None, None, None, None),
        P(None, "lat", "lon", None),
    )
    return jax.shard_map(
        on_device,
        mesh=mesh,
        in_specs=placed,
        out_specs=(
            P(None, "lat", "lon", None),
            P(None, "lat", "lon", None),
            P(),
            P(),
            P(),
            P(),
            P("lat", None, None, None, None),
        ),
        check_vma=False,
    )
```

```python
import functools
import math

import jax
import jax.numpy as jnp
import numpy as np
from jax import lax
from jax.experimental import pallas as pl
from jax.experimental.pallas import tpu as pltpu
from jax.sharding import PartitionSpec as P

WA = 12
WO = 12
HALF = 6
HEADS = 6
HEAD = 32
WIN = WA * WO
SPAN = 2 * WO - 1
CUT = WA * SPAN
WIDE = 384
LANES = 128
C = 192
HID = 768
TOKENS = 576
PARTS = 4
PACKED = 1792
SOURCES = 768
INNER = 2 * WO - HALF
LONG = 2 * HALF * INNER
SHORT = 2 * HALF * HALF
MAIN = HEADS * WA
BIAS_ROWS = 176
LEFT = CUT - 2 * LANES
EPS = 1e-05
SCALE = HEAD ** (-0.5)
LARGE = 28 * 1024 * 1024
SMALL = 12 * 1024 * 1024
BF = jnp.bfloat16
F32 = jnp.float32


def table_order():
    lane = np.arange(CUT)
    order = np.zeros((CUT, WIDE), np.float32)
    order[(lane % WA) * SPAN + SPAN - 1 - lane // WA, lane] = 1.0
    return order


def table_back():
    back = np.zeros((2, WIDE, 2 * CUT), np.float32)
    for level in range(2):
        back[level, :, level * CUT : (level + 1) * CUT] = table_order().T
    return back


def window_order():
    order = np.zeros((TOKENS, SOURCES), np.float32)
    near, far = 2 * HALF * 2 * WO, 2 * HALF * 8
    for window, level, column, row in np.ndindex(2, 2, WO, WA):
        token = ((window * 2 + level) * WO + column) * WA + row
        place, across = (1 - level) * HALF + row % HALF, window * WO + column + HALF
        inside = across < 2 * WO
        at = place * 2 * WO + across if inside else 2 * near + place * 8 + across - 2 * WO
        if row >= HALF:
            at += near if inside else far
        order[token, at] = 1.0
    return order


def piece_row(level, row, column):
    place, inside = level * HALF + row % HALF, column >= HALF
    at = place * INNER + column - HALF if inside else 2 * LONG + place * HALF + column
    return at + (0 if row >= HALF else LONG if inside else SHORT)


def split_order():
    order = np.zeros((TOKENS, TOKENS), np.float32)
    for window, level, column, row in np.ndindex(2, 2, WO, WA):
        token = ((window * 2 + level) * WO + column) * WA + row
        across = (window * WO + column + HALF) % (2 * WO)
        order[piece_row(1 - level, (row + HALF) % WA, across), token] = 1.0
    return order


def join_order():
    order = np.zeros((TOKENS, TOKENS), np.float32)
    for level, row, column in np.ndindex(2, WA, 2 * WO):
        order[(level * WA + row) * 2 * WO + column, piece_row(level, row, column)] = 1.0
    return order


def dot(a, b):
    return jnp.dot(a, b, preferred_element_type=F32)


def dot_rt(a, b):
    return lax.dot_general(a, b, (((1,), (1,)), ((), ())), preferred_element_type=F32)


def dot_lt(a, b):
    return lax.dot_general(a, b, (((0,), (0,)), ((), ())), preferred_element_type=F32)


def row_mean(values, exact=False):
    ones = jnp.full((C, C), 1.0, BF)
    high = values.astype(BF)
    total = dot(high, ones)
    if not exact:
        total = total + dot((values - high.astype(F32)).astype(BF), ones)
    return total * (1.0 / C)


def normal(values, mean):
    centred = values - mean
    inverse = lax.rsqrt(row_mean(centred * centred) + EPS)
    return centred * inverse, inverse


def normal_back(unit, inverse, grad):
    first = row_mean(grad, exact=True)
    second = row_mean(grad * unit)
    return inverse * (grad - first - unit * second)


def halo_kernel(tokens_ref, cot_ref, below_ref, beside_ref, corner_ref):
    for array, ref in enumerate((tokens_ref, cot_ref)):
        for level in range(2):
            for row in range(HALF):
                below_ref[array, level, row] = ref[level, row]
                beside_ref[array, level, row] = ref[level, row + HALF].astype(F32)[:8].astype(BF)
                corner_ref[array, level, row] = ref[level, row].astype(F32)[:8].astype(BF)


def bias_kernel(last_ref, table_ref, bias_ref):
    table = table_ref[0, 0].reshape(HEADS * 2 * WA, 2 * CUT)
    high = table.astype(BF)
    rest = table - high.astype(F32)
    middle = rest.astype(BF)
    low = (rest - middle.astype(F32)).astype(BF)
    lane = lax.broadcasted_iota(jnp.int32, (1, WIDE), 1)
    source = jnp.where(lane < CUT, lane % WA * SPAN + SPAN - 1 - lane // WA, -2 * CUT)
    place = lax.broadcasted_iota(jnp.int32, (2 * CUT, WIDE), 0)
    row = lax.broadcasted_iota(jnp.int32, (2 * WA, WIDE), 0)
    row_i = lax.broadcasted_iota(jnp.int32, (2 * WA, WIN), 0) % WA
    row_j = lax.broadcasted_iota(jnp.int32, (2 * WA, WIN), 1) % WA
    split = (row_i >= HALF) != (row_j >= HALF)
    split = jnp.logical_and(split, last_ref[0] == 1)
    for level in range(2):
        order = (place == source + level * CUT).astype(F32).astype(BF)
        wide = sum(dot(term, order) for term in (low, middle, high))
        for head in range(HEADS):
            both = wide[head * 2 * WA : (head + 1) * 2 * WA]
            other = pltpu.roll(both, WA, 0)
            upper, lower = (other, both) if level else (both, other)
            both = jnp.where(row < WA, pltpu.roll(upper, WIDE - WA, 1), lower)
            blocks = []
            for pair in range(WO // 2):
                turn = (WO - 2 - 2 * pair) * WA
                block = pltpu.roll(both, (WIDE - turn) % WIDE, 1)[:, :WIN]
                blocks.append(jnp.where(split, -1e30, block))
            block = jnp.transpose(jnp.concatenate(blocks, axis=0))
            bias_ref[level, head * WIN : (head + 1) * WIN, :] = block


def block_kernel(
    core_ref, tokens_ref, cots_ref, below_ref, beside_ref, corner_ref, order_ref,
    qkv_ref, proj_ref, up_ref, down_ref, bias_ref,
    mine_ref, other_ref, ds_ref, act_ref, res_ref, gres_ref, dq_ref, dk_ref, dv_ref, unit_ref, inverse_ref,
    source_ref, x_ref, cot_ref, normed_ref, q_ref, k_ref, v_ref, prob_ref, att_ref, two_ref, upper_ref, gact_ref,
    gup_ref, gmix_ref, gatt_ref, turned_ref, unit_two_ref, inverse_two_ref, mean_ref,
):
    lane = lax.broadcasted_iota(jnp.int32, (1, C), 1) // HEAD
    half_masks = [(lane == head).astype(F32).astype(BF) for head in range(HEADS)]

    def rows_of(part):
        return pl.ds(pl.multiple_of(part * WIN, WIN), WIN)

    near, far = 2 * HALF * 2 * WO, 2 * HALF * 8
    for array, (ref, target) in enumerate(((tokens_ref, x_ref), (cots_ref, cot_ref))):
        for level in range(2):
            for row in range(HALF):
                place = level * HALF + row
                at = place * 2 * WO
                source_ref[at : at + 2 * WO, :] = ref[level, row + HALF].astype(F32)
                source_ref[near + at : near + at + 2 * WO, :] = below_ref[array, level, row].astype(F32)
                at = 2 * near + place * 8
                source_ref[at : at + 8, :] = beside_ref[array, level, row].astype(F32)
                source_ref[far + at : far + at + 8, :] = corner_ref[array, level, row].astype(F32)
        target[...] = dot(order_ref[...], source_ref[...].astype(BF)).astype(BF)

    def first_norm(part, carry):
        rows = rows_of(part)
        mean = row_mean(x_ref[rows, :], exact=True)
        unit, inverse = normal(x_ref[rows, :].astype(F32), mean)
        mean_ref[rows, :] = mean
        unit_ref[rows, :] = unit
        inverse_ref[rows, :] = inverse
        normed_ref[rows, :] = unit.astype(BF)
        return carry

    lax.fori_loop(0, PARTS, first_norm, 0, unroll=4)
    normed = normed_ref[...]
    weights = [qkv_ref[:, part * C : (part + 1) * C] for part in range(3)]
    for target, weight in zip((q_ref, k_ref, v_ref), weights):
        target[...] = dot(normed, weight).astype(BF)

    def attend(part, carry):
        rows = rows_of(part)
        query, key, value = q_ref[rows, :], k_ref[rows, :], v_ref[rows, :]
        level = part % 2
        value_t = jnp.transpose(value)
        chunks = [slice(head * WIN, (head + 1) * WIN) for head in range(HEADS)]
        scores = [dot_rt(key * mask, query) for mask in half_masks]
        for head, chunk in enumerate(chunks):
            score = scores[head] * SCALE + bias_ref[level, chunk, :]
            exponent = jnp.exp(score - jnp.max(score, axis=0, keepdims=True))
            prob = exponent * (1.0 / jnp.sum(exponent, axis=0, keepdims=True))
            prob_ref[part, chunk, :] = prob.astype(BF)
        for head, chunk in enumerate(chunks):
            own = slice(head * HEAD, (head + 1) * HEAD)
            turned_ref[own, :] = dot(value_t[own], prob_ref[part, chunk, :])
        att_ref[rows, :] = jnp.transpose(turned_ref[...]).astype(BF)
        return carry

    lax.fori_loop(0, PARTS, attend, 0, unroll=4)
    res_ref[...] = dot(att_ref[...], proj_ref[...])

    def second_norm(part, carry):
        rows = rows_of(part)
        mixed = res_ref[rows, :].astype(BF)
        residual = x_ref[rows, :].astype(F32) + mixed.astype(F32)
        res_ref[rows, :] = residual
        unit, inverse = normal(residual, mean_ref[rows, :] + row_mean(mixed, exact=True))
        unit_two_ref[rows, :] = unit
        inverse_two_ref[rows, :] = inverse
        two_ref[rows, :] = unit.astype(BF)
        return carry

    lax.fori_loop(0, PARTS, second_norm, 0, unroll=4)
    upper_ref[...] = dot(two_ref[...], up_ref[...])
    gact_ref[...] = dot(cot_ref[...], down_ref[...]).astype(BF)
    step = 32

    def gelu(chunk, carry):
        rows = pl.ds(pl.multiple_of(chunk * step, step), step)
        upper = upper_ref[rows, :]
        cdf = 0.5 + 0.5 * lax.erf(upper * math.sqrt(0.5))
        pdf = jnp.exp(upper * upper * -0.5) * (1.0 / math.sqrt(2.0 * math.pi))
        act_ref[rows, :] = (upper * cdf).astype(BF)
        gup_ref[rows, :] = (gact_ref[rows, :].astype(F32) * (cdf + upper * pdf)).astype(BF)
        return carry

    lax.fori_loop(0, TOKENS // step, gelu, 0)
    gres_ref[...] = dot_rt(gup_ref[...], up_ref[...])

    def second_back(part, carry):
        rows = rows_of(part)
        unit, inverse = unit_two_ref[rows, :], inverse_two_ref[rows, :]
        grad = gres_ref[rows, :].astype(BF).astype(F32)
        grad = cot_ref[rows, :].astype(F32) + normal_back(unit, inverse, grad)
        gres_ref[rows, :] = grad
        gmix_ref[rows, :] = grad.astype(BF)
        return carry

    lax.fori_loop(0, PARTS, second_back, 0, unroll=4)
    gatt_ref[...] = dot_rt(gmix_ref[...], proj_ref[...]).astype(BF)
    ds_ref[...] = jnp.zeros(ds_ref.shape, F32)

    def attend_back(part, carry):
        rows = rows_of(part)
        query, key, value = q_ref[rows, :], k_ref[rows, :], v_ref[rows, :]
        gatt = gatt_ref[rows, :]
        level = part % 2
        key_t = jnp.transpose(key)
        chunks = [slice(head * WIN, (head + 1) * WIN) for head in range(HEADS)]
        gowns = [gatt * mask for mask in half_masks]
        gprobs = [dot_rt(value, gown) for gown in gowns]
        gscores = []
        for head, chunk in enumerate(chunks):
            weight = prob_ref[part, chunk, :].astype(F32)
            gscore = weight * (gprobs[head] - jnp.sum(weight * gprobs[head], axis=0, keepdims=True))
            ds_ref[level, chunk, :] += gscore
            gscores.append(gscore.astype(BF))
        gkey = jnp.zeros((WIN, C), F32)
        gvalue = jnp.zeros((WIN, C), F32)
        for head, chunk in enumerate(chunks):
            own = slice(head * HEAD, (head + 1) * HEAD)
            turned_ref[own, :] = dot(key_t[own], gscores[head])
            gkey = gkey + dot(gscores[head], query * half_masks[head])
            gvalue = gvalue + dot(prob_ref[part, chunk, :], gowns[head])
        dq_ref[rows, :] = (jnp.transpose(turned_ref[...]) * SCALE).astype(BF)
        dk_ref[rows, :] = (gkey * SCALE).astype(BF)
        dv_ref[rows, :] = gvalue.astype(BF)
        return carry

    lax.fori_loop(0, PARTS, attend_back, 0, unroll=4)
    first = core_ref[0] == 0

    def put(start, zero, one):
        rows = slice(start, start + zero.shape[0])
        mine_ref[rows, :] = jnp.where(first, zero, one)
        other_ref[rows, :] = jnp.where(first, one, zero).astype(BF)

    gup = dot_lt(two_ref[...], gup_ref[...])
    gdown = dot_lt(cot_ref[...], act_ref[...])
    for chunk in range(6):
        columns = slice(chunk * LANES, (chunk + 1) * LANES)
        put(chunk * C, gup[:, columns], gdown[:, columns])
    normed = normed_ref[...]
    gq = dot_lt(normed, dq_ref[...])
    gk = dot_lt(normed, dk_ref[...])
    gv = dot_lt(normed, dv_ref[...])
    gproj = dot_lt(att_ref[...], gmix_ref[...])
    put(6 * C, gq[:, :LANES], gproj[:, :LANES])
    put(7 * C, gk[:, :LANES], jnp.concatenate([gq[:, LANES:], gk[:, LANES:]], axis=1))
    put(8 * C, gv[:, :LANES], jnp.concatenate([gv[:, LANES:], gproj[:, LANES:]], axis=1))
    mine_ref[9 * C :, :] = jnp.zeros((PACKED - 9 * C, LANES), F32)
    other_ref[9 * C :, :] = jnp.zeros((PACKED - 9 * C, LANES), BF)


def table_kernel(ds_ref, gbias_ref, bsum_ref):
    row = lax.broadcasted_iota(jnp.int32, (2 * WA, WIDE), 0)

    def table_grad(level, head):
        scores = jnp.transpose(ds_ref[level, head * WIN : (head + 1) * WIN, :])
        total = jnp.zeros((2 * WA, WIDE), F32)
        for pair in range(WO // 2):
            turn = (WO - 2 - 2 * pair) * WA
            block = scores[pair * 2 * WA : (pair + 1) * 2 * WA]
            block = jnp.concatenate([block, jnp.zeros((2 * WA, WIDE - WIN), F32)], axis=1)
            total = total + (pltpu.roll(block, turn, 1) if turn else block)
        total = jnp.where(row < WA, pltpu.roll(total, WA, 1), total)
        return total + pltpu.roll(total, WA, 0)

    for level in range(2):
        left = jnp.zeros((2 * WA, LANES), F32)
        for pair in range(HEADS // 2):
            both = jnp.where(row < WA, table_grad(level, 2 * pair), table_grad(level, 2 * pair + 1))
            start = pair * 2 * WA
            bsum_ref[level, start : start + 2 * WA, :] = both[:, :LANES]
            bsum_ref[level, MAIN + start : MAIN + start + 2 * WA, :] = both[:, LANES : 2 * LANES]
            rest = both[:, 2 * LANES :]
            left = left + (pltpu.roll(rest, pair * LEFT, 1) if pair else rest)
        bsum_ref[level, 2 * MAIN : 2 * MAIN + 2 * WA, :] = left
        bsum_ref[level, 2 * MAIN + 2 * WA :, :] = jnp.zeros((BIAS_ROWS - 2 * MAIN - 2 * WA, LANES), F32)
    gbias_ref[...] = bsum_ref[...].reshape(2 * BIAS_ROWS, LANES).astype(BF)


def added(one, two):
    return (one.astype(F32) + two.astype(F32)).astype(BF)


def first_kernel(mine_ref, got_ref, own_ref, came_ref, wait_ref, sum_ref, bias_ref):
    sum_ref[...] = (mine_ref[...] + got_ref[...].astype(F32)).astype(BF)
    bias_ref[...] = added(own_ref[...], came_ref[...])


def middle_kernel(got_ref, own_ref, came_ref, wait_ref, wide_ref, bias_ref):
    total = jnp.sum(got_ref[...].astype(F32), axis=0).astype(BF)
    for block in range(wide_ref.shape[0]):
        wide_ref[block] = total
    bias_ref[...] = added(own_ref[...], came_ref[...])


def late_kernel(
    act_ref, res_ref, gres_ref, dq_ref, dk_ref, dv_ref, unit_ref, inverse_ref, qkv_ref, down_ref, order_ref,
    own_ref, above_ref, beside_ref, corner_ref, grad_ref,
):
    result = (res_ref[...] + dot_rt(act_ref[...], down_ref[...])).astype(BF)
    grads = (dq_ref, dk_ref, dv_ref)
    grad_ref[...] = sum(dot_rt(ref[...], qkv_ref[:, i * C : (i + 1) * C]) for i, ref in enumerate(grads))

    def first_back(part, carry):
        rows = pl.ds(pl.multiple_of(part * WIN, WIN), WIN)
        grad = grad_ref[rows, :].astype(BF).astype(F32)
        grad_ref[rows, :] = gres_ref[rows, :] + normal_back(unit_ref[rows, :], inverse_ref[rows, :], grad)
        return carry

    lax.fori_loop(0, PARTS, first_back, 0, unroll=4)
    order = order_ref[...]
    rows = jnp.concatenate([dot(order, result), dot(order, grad_ref[...].astype(BF))], axis=1)
    start = 0
    for ref in (own_ref, above_ref, beside_ref, corner_ref):
        ref[...] = rows[start : start + ref.shape[0]].astype(BF)
        start += ref.shape[0]


def join_kernel(own_ref, above_ref, beside_ref, corner_ref, order_ref, result_ref, gtok_ref):
    pieces = [ref[...].astype(F32) for ref in (own_ref, above_ref, beside_ref, corner_ref)]
    rows = dot(order_ref[...], jnp.concatenate(pieces, axis=0).astype(BF))
    for array, ref in enumerate((result_ref, gtok_ref)):
        part = rows[:, array * C : (array + 1) * C]
        for level in range(2):
            for row in range(WA):
                at = (level * WA + row) * 2 * WO
                ref[level, row] = part[at : at + 2 * WO].astype(BF)


def final_kernel(
    count, core_ref, mine_ref, other_ref, gbias_ref, back_ref,
    qkv_ref, proj_ref, up_ref, down_ref, bias_ref,
):
    first = core_ref[0] == 0
    squares = jnp.zeros((C, LANES), F32)
    for place in range(9):
        for ref in (mine_ref, other_ref):
            part = ref[place * C : (place + 1) * C, :].astype(F32)
            squares = squares + part * part
    total = jnp.sum(squares)
    factor = jnp.minimum(1.0, math.sqrt(count) / (jnp.sqrt(jnp.full((8, LANES), total)) + 1e-06))[:1]

    def chunk(half, place):
        rows = slice(place * C, (place + 1) * C)
        mine, other = mine_ref[rows, :].astype(F32), other_ref[rows, :].astype(F32)
        return (jnp.where(first, other, mine) if half else jnp.where(first, mine, other)) * factor

    for place in range(6):
        up_ref[:, place * LANES : (place + 1) * LANES] = chunk(0, place)
        down_ref[:, place * LANES : (place + 1) * LANES] = chunk(1, place)
    last = C - LANES
    left, right = chunk(1, 7), chunk(1, 8)
    qkv_ref[:, :C] = jnp.concatenate([chunk(0, 6), left[:, :last]], axis=1)
    qkv_ref[:, C : 2 * C] = jnp.concatenate([chunk(0, 7), left[:, last:]], axis=1)
    qkv_ref[:, 2 * C :] = jnp.concatenate([chunk(0, 8), right[:, :last]], axis=1)
    proj_ref[...] = jnp.concatenate([chunk(1, 6), right[:, last:]], axis=1)

    sums = gbias_ref[...].astype(F32)
    tables = []
    for level in range(2):
        packed = sums[level * BIAS_ROWS : (level + 1) * BIAS_ROWS]
        left = packed[2 * MAIN : 2 * MAIN + 2 * WA]
        left = [left] + [pltpu.roll(left, LANES - pair * LEFT, 1) for pair in range(1, HEADS // 2)]
        rows = [packed[:MAIN], packed[MAIN : 2 * MAIN], jnp.concatenate(left, axis=0)]
        rows = jnp.concatenate(rows, axis=1).astype(BF)
        tables.append(dot(rows, back_ref[level]) * factor[:, :1])
    row = lax.broadcasted_iota(jnp.int32, (2 * WA, 2 * CUT), 0)
    for pair in range(HEADS // 2):
        upper, lower = [table[pair * 2 * WA : (pair + 1) * 2 * WA] for table in tables]
        bias_ref[0, 0, 2 * pair] = jnp.where(row < WA, upper, pltpu.roll(lower, WA, 0))
        bias_ref[0, 0, 2 * pair + 1] = jnp.where(row < WA, pltpu.roll(upper, WA, 0), lower)


def call(kernel, outs, scalars, arrays, scratch=(), limit=SMALL):
    spaces = [pl.BlockSpec(memory_space=pltpu.SMEM)] * scalars
    spaces += [pl.BlockSpec(memory_space=pltpu.VMEM)] * arrays
    return pl.pallas_call(
        kernel,
        out_shape=outs,
        in_specs=spaces,
        out_specs=[pl.BlockSpec(memory_space=pltpu.VMEM)] * len(outs),
        scratch_shapes=scratch,
        compiler_params=pltpu.CompilerParams(vmem_limit_bytes=limit),
    )


def shape(*sizes, kind=F32):
    return jax.ShapeDtypeStruct(sizes, kind)


def from_next(block, axes, distance):
    sizes = [lax.axis_size(axis) for axis in axes]
    route = []
    for place in np.ndindex(*sizes):
        source = [(i + distance) % size for i, size in zip(place, sizes)]
        route.append((int(np.ravel_multi_index(source, sizes)), int(np.ravel_multi_index(place, sizes))))
    return lax.ppermute(block, tuple(axes), route)


def roll_back_start(*arrays):
    outs = [shape(rows, 2 * C, kind=BF) for rows in (LONG, LONG, SHORT, SHORT)]
    order = jnp.asarray(split_order(), BF)
    pieces = call(late_kernel, outs, 0, 11, [pltpu.VMEM((TOKENS, C), F32)])(*arrays, order)
    own, above, beside, corner = pieces
    above = from_next(above, ["lat"], -1)
    corner = from_next(corner, ["lat", "lon"], -1)
    beside = from_next(beside, ["lon"], -1)
    return own, above, beside, corner


def roll_back_end(pieces):
    whole = shape(2, WA, 2 * WO, C, kind=BF)
    return call(join_kernel, [whole, whole], 0, 5)(*pieces, jnp.asarray(join_order(), BF))


def gradient_sums(mine, other, bias, pieces):
    lat, lon = lax.axis_size("lat"), lax.axis_size("lon")
    half, depth = lat // 2, lon // 2
    pairs = [(i, i ^ 1) for i in range(lat)]
    planes = [
        [(2 * i + core) * lon + 2 * z + low for i in range(half) for low in range(2)]
        for core in range(2)
        for z in range(depth)
    ]
    columns = [[2 * z + low for z in range(depth)] for low in range(2)]
    share = PACKED // lat

    def partner(block, distance):
        return lax.ppermute(block, "lon", [(i, i ^ distance) for i in range(lon)])

    def middle(got, own, came, blocks, wait):
        outs = [shape(blocks, share, LANES, kind=BF), shape(2 * BIAS_ROWS, LANES, kind=BF)]
        return call(middle_kernel, outs, 0, 4)(got, own, came, wait)

    own, above, beside, corner = pieces
    outs = [shape(PACKED, LANES, kind=BF), shape(2 * BIAS_ROWS, LANES, kind=BF)]
    got = lax.ppermute(other, "lat", pairs)
    mine, bias = call(first_kernel, outs, 0, 5)(mine, got, bias, partner(bias, 2), own[:8, :LANES])
    got = lax.all_to_all(mine.reshape(lat, share, LANES), ("lat", "lon"), 0, 0, axis_index_groups=planes)
    wide, bias = middle(got, bias, partner(bias, 4), depth, corner[:8, :LANES])
    got = lax.all_to_all(wide, "lon", 0, 0, axis_index_groups=columns)
    wide, bias = middle(got, bias, partner(bias, 1), lat, above[:8, :LANES])
    bias = added(bias, partner(bias, 8))
    mine = lax.all_to_all(wide, ("lat", "lon"), 0, 0, axis_index_groups=planes)
    wait = added(bias[:8], beside[:8, :LANES])
    mine = lax.dynamic_update_slice(mine, wait[None], (lat - 1, share - 8, 0))
    other = lax.ppermute(mine, "lat", pairs)
    return mine.reshape(PACKED, LANES), other.reshape(PACKED, LANES), bias


def on_device(tokens, w_qkv, w_proj, w_up, w_down, earth_bias, cotangent):
    band = lax.axis_index("lat")
    bands = lax.axis_size("lat")
    core = (band % 2).astype(jnp.int32).reshape(1)
    last = (band == bands - 1).astype(jnp.int32).reshape(1)

    wide, narrow = shape(2, 2, HALF, 2 * WO, C, kind=BF), shape(2, 2, HALF, 8, C, kind=BF)
    below, beside, corner = call(halo_kernel, [wide, narrow, narrow], 0, 2)(tokens, cotangent)
    below = from_next(below, ["lat"], 1)
    corner = from_next(corner, ["lat", "lon"], 1)
    beside = from_next(beside, ["lon"], 1)
    back = table_back()
    bias = call(bias_kernel, [shape(2, HEADS * WIN, WIN)], 1, 1)(last, earth_bias)[0]

    def tokens_of(width, kind=BF):
        return pltpu.VMEM((TOKENS, width), kind)

    outs = [shape(PACKED, LANES), shape(PACKED, LANES, kind=BF), shape(2, HEADS * WIN, WIN)]
    outs += [shape(TOKENS, HID, kind=BF), shape(TOKENS, C), shape(TOKENS, C)]
    outs += [shape(TOKENS, C, kind=BF)] * 3 + [shape(TOKENS, C)] * 2
    scratch = [pltpu.VMEM((SOURCES, C), F32)] + [tokens_of(C)] * 6
    scratch += [pltpu.VMEM((PARTS, HEADS * WIN, WIN), BF), tokens_of(C), tokens_of(C), tokens_of(HID, F32)]
    scratch += [tokens_of(HID)] * 2 + [tokens_of(C)] * 2 + [pltpu.VMEM((C, WIN), F32)] + [tokens_of(C, F32)] * 3
    mine, other, scores, *late = call(block_kernel, outs, 1, 11, scratch, limit=LARGE)(
        core, tokens, cotangent, below, beside, corner, jnp.asarray(window_order(), BF),
        w_qkv, w_proj, w_up, w_down.T, bias,
    )
    scratch = [pltpu.VMEM((2, BIAS_ROWS, LANES), F32)]
    grad_table = call(table_kernel, [shape(2 * BIAS_ROWS, LANES, kind=BF)], 0, 1, scratch)(scores)[0]
    pieces = roll_back_start(*late, w_qkv, w_down.T)
    sums = gradient_sums(mine, other, grad_table, pieces)
    result, grad_tokens = roll_back_end(pieces)

    count = w_qkv.size + w_proj.size + w_up.size + w_down.size + earth_bias.size * bands
    outs = [shape(C, 3 * C), shape(C, C), shape(C, HID), shape(C, HID), shape(1, 1, HEADS, 2 * WA, 2 * CUT)]
    grads = call(functools.partial(final_kernel, count), outs, 1, 4)(core, *sums, jnp.asarray(back, BF))
    return (result, grad_tokens, *grads[:3], grads[3].T, grads[4])


def solution(mesh):
    placed = (
        P(None, "lat", "lon", None),
        P(),
        P(),
        P(),
        P(),
        P("lat", None, None, None, None),
        P(None, "lat", "lon", None),
    )
    return jax.shard_map(
        on_device,
        mesh=mesh,
        in_specs=placed,
        out_specs=(
            P(None, "lat", "lon", None),
            P(None, "lat", "lon", None),
            P(),
            P(),
            P(),
            P(),
            P("lat", None, None, None, None),
        ),
        check_vma=False,
    )
```

```python
import functools
import math

import jax
import jax.numpy as jnp
import numpy as np
from jax import lax
from jax.experimental import pallas as pl
from jax.experimental.pallas import tpu as pltpu
from jax.sharding import PartitionSpec as P

WA = 12
WO = 12
HALF = 6
HEADS = 6
HEAD = 32
WIN = WA * WO
SPAN = 2 * WO - 1
CUT = WA * SPAN
WIDE = 384
LANES = 128
C = 192
HID = 768
TOKENS = 576
PARTS = 4
PACKED = 1792
SOURCES = 768
INNER = 2 * WO - HALF
LONG = 2 * HALF * INNER
SHORT = 2 * HALF * HALF
MAIN = HEADS * WA
BIAS_ROWS = 176
LEFT = CUT - 2 * LANES
EPS = 1e-05
SCALE = HEAD ** (-0.5)
LARGE = 28 * 1024 * 1024
SMALL = 12 * 1024 * 1024
BF = jnp.bfloat16
F32 = jnp.float32


def table_order():
    lane = np.arange(CUT)
    order = np.zeros((CUT, WIDE), np.float32)
    order[(lane % WA) * SPAN + SPAN - 1 - lane // WA, lane] = 1.0
    return order


def table_back():
    back = np.zeros((2, WIDE, 2 * CUT), np.float32)
    for level in range(2):
        back[level, :, level * CUT : (level + 1) * CUT] = table_order().T
    return back


def window_order():
    order = np.zeros((TOKENS, SOURCES), np.float32)
    near, far = 2 * HALF * 2 * WO, 2 * HALF * 8
    for window, level, column, row in np.ndindex(2, 2, WO, WA):
        token = ((window * 2 + level) * WO + column) * WA + row
        place, across = (1 - level) * HALF + row % HALF, window * WO + column + HALF
        inside = across < 2 * WO
        at = place * 2 * WO + across if inside else 2 * near + place * 8 + across - 2 * WO
        if row >= HALF:
            at += near if inside else far
        order[token, at] = 1.0
    return order


def piece_row(level, row, column):
    place, inside = level * HALF + row % HALF, column >= HALF
    at = place * INNER + column - HALF if inside else 2 * LONG + place * HALF + column
    return at + (0 if row >= HALF else LONG if inside else SHORT)


def split_order():
    order = np.zeros((TOKENS, TOKENS), np.float32)
    for window, level, column, row in np.ndindex(2, 2, WO, WA):
        token = ((window * 2 + level) * WO + column) * WA + row
        across = (window * WO + column + HALF) % (2 * WO)
        order[piece_row(1 - level, (row + HALF) % WA, across), token] = 1.0
    return order


def join_order():
    order = np.zeros((TOKENS, TOKENS), np.float32)
    for level, row, column in np.ndindex(2, WA, 2 * WO):
        order[(level * WA + row) * 2 * WO + column, piece_row(level, row, column)] = 1.0
    return order


def dot(a, b):
    return jnp.dot(a, b, preferred_element_type=F32)


def dot_rt(a, b):
    return lax.dot_general(a, b, (((1,), (1,)), ((), ())), preferred_element_type=F32)


def dot_lt(a, b):
    return lax.dot_general(a, b, (((0,), (0,)), ((), ())), preferred_element_type=F32)


def row_mean(values, exact=False):
    ones = jnp.full((C, C), 1.0, BF)
    high = values.astype(BF)
    total = dot(high, ones)
    if not exact:
        total = total + dot((values - high.astype(F32)).astype(BF), ones)
    return total * (1.0 / C)


def normal(values, mean):
    centred = values - mean
    inverse = lax.rsqrt(row_mean(centred * centred) + EPS)
    return centred * inverse, inverse


def normal_back(unit, inverse, grad):
    first = row_mean(grad, exact=True)
    second = row_mean(grad * unit)
    return inverse * (grad - first - unit * second)


def halo_kernel(tokens_ref, cot_ref, below_ref, beside_ref, corner_ref):
    for array, ref in enumerate((tokens_ref, cot_ref)):
        for level in range(2):
            for row in range(HALF):
                below_ref[array, level, row] = ref[level, row]
                beside_ref[array, level, row] = ref[level, row + HALF].astype(F32)[:8].astype(BF)
                corner_ref[array, level, row] = ref[level, row].astype(F32)[:8].astype(BF)


def bias_kernel(last_ref, table_ref, bias_ref):
    table = table_ref[0, 0].reshape(HEADS * 2 * WA, 2 * CUT)
    high = table.astype(BF)
    rest = table - high.astype(F32)
    middle = rest.astype(BF)
    low = (rest - middle.astype(F32)).astype(BF)
    lane = lax.broadcasted_iota(jnp.int32, (1, WIDE), 1)
    source = jnp.where(lane < CUT, lane % WA * SPAN + SPAN - 1 - lane // WA, -2 * CUT)
    place = lax.broadcasted_iota(jnp.int32, (2 * CUT, WIDE), 0)
    row = lax.broadcasted_iota(jnp.int32, (2 * WA, WIDE), 0)
    row_i = lax.broadcasted_iota(jnp.int32, (2 * WA, WIN), 0) % WA
    row_j = lax.broadcasted_iota(jnp.int32, (2 * WA, WIN), 1) % WA
    split = (row_i >= HALF) != (row_j >= HALF)
    split = jnp.logical_and(split, last_ref[0] == 1)
    for level in range(2):
        order = (place == source + level * CUT).astype(F32).astype(BF)
        wide = sum(dot(term, order) for term in (low, middle, high))
        for head in range(HEADS):
            both = wide[head * 2 * WA : (head + 1) * 2 * WA]
            other = pltpu.roll(both, WA, 0)
            upper, lower = (other, both) if level else (both, other)
            both = jnp.where(row < WA, pltpu.roll(upper, WIDE - WA, 1), lower)
            blocks = []
            for pair in range(WO // 2):
                turn = (WO - 2 - 2 * pair) * WA
                block = pltpu.roll(both, (WIDE - turn) % WIDE, 1)[:, :WIN]
                blocks.append(jnp.where(split, -1e30, block))
            block = jnp.transpose(jnp.concatenate(blocks, axis=0))
            bias_ref[level, head * WIN : (head + 1) * WIN, :] = block


def block_kernel(
    core_ref, tokens_ref, cots_ref, below_ref, beside_ref, corner_ref, order_ref,
    qkv_ref, proj_ref, up_ref, down_ref, bias_ref,
    mine_ref, other_ref, gbias_ref, act_ref, res_ref, gres_ref, dq_ref, dk_ref, dv_ref, unit_ref, inverse_ref,
    source_ref, x_ref, cot_ref, normed_ref, q_ref, k_ref, v_ref, prob_ref, att_ref, two_ref, upper_ref, gact_ref,
    gup_ref, gmix_ref, gatt_ref, ds_ref, bsum_ref, turned_ref, unit_two_ref, inverse_two_ref, mean_ref,
):
    lane = lax.broadcasted_iota(jnp.int32, (1, C), 1) // HEAD
    half_masks = [(lane == head).astype(F32).astype(BF) for head in range(HEADS)]

    def rows_of(part):
        return pl.ds(pl.multiple_of(part * WIN, WIN), WIN)

    near, far = 2 * HALF * 2 * WO, 2 * HALF * 8
    for array, (ref, target) in enumerate(((tokens_ref, x_ref), (cots_ref, cot_ref))):
        for level in range(2):
            for row in range(HALF):
                place = level * HALF + row
                at = place * 2 * WO
                source_ref[at : at + 2 * WO, :] = ref[level, row + HALF].astype(F32)
                source_ref[near + at : near + at + 2 * WO, :] = below_ref[array, level, row].astype(F32)
                at = 2 * near + place * 8
                source_ref[at : at + 8, :] = beside_ref[array, level, row].astype(F32)
                source_ref[far + at : far + at + 8, :] = corner_ref[array, level, row].astype(F32)
        target[...] = dot(order_ref[...], source_ref[...].astype(BF)).astype(BF)

    def first_norm(part, carry):
        rows = rows_of(part)
        mean = row_mean(x_ref[rows, :], exact=True)
        unit, inverse = normal(x_ref[rows, :].astype(F32), mean)
        mean_ref[rows, :] = mean
        unit_ref[rows, :] = unit
        inverse_ref[rows, :] = inverse
        normed_ref[rows, :] = unit.astype(BF)
        return carry

    lax.fori_loop(0, PARTS, first_norm, 0, unroll=4)
    normed = normed_ref[...]
    weights = [qkv_ref[:, part * C : (part + 1) * C] for part in range(3)]
    for target, weight in zip((q_ref, k_ref, v_ref), weights):
        target[...] = dot(normed, weight).astype(BF)

    def attend(part, carry):
        rows = rows_of(part)
        query, key, value = q_ref[rows, :], k_ref[rows, :], v_ref[rows, :]
        level = part % 2
        value_t = jnp.transpose(value)
        chunks = [slice(head * WIN, (head + 1) * WIN) for head in range(HEADS)]
        scores = [dot_rt(key * mask, query) for mask in half_masks]
        for head, chunk in enumerate(chunks):
            score = scores[head] * SCALE + bias_ref[level, chunk, :]
            exponent = jnp.exp(score - jnp.max(score, axis=0, keepdims=True))
            prob = exponent * (1.0 / jnp.sum(exponent, axis=0, keepdims=True))
            prob_ref[part, chunk, :] = prob.astype(BF)
        for head, chunk in enumerate(chunks):
            own = slice(head * HEAD, (head + 1) * HEAD)
            turned_ref[own, :] = dot(value_t[own], prob_ref[part, chunk, :])
        att_ref[rows, :] = jnp.transpose(turned_ref[...]).astype(BF)
        return carry

    lax.fori_loop(0, PARTS, attend, 0, unroll=4)
    res_ref[...] = dot(att_ref[...], proj_ref[...])

    def second_norm(part, carry):
        rows = rows_of(part)
        mixed = res_ref[rows, :].astype(BF)
        residual = x_ref[rows, :].astype(F32) + mixed.astype(F32)
        res_ref[rows, :] = residual
        unit, inverse = normal(residual, mean_ref[rows, :] + row_mean(mixed, exact=True))
        unit_two_ref[rows, :] = unit
        inverse_two_ref[rows, :] = inverse
        two_ref[rows, :] = unit.astype(BF)
        return carry

    lax.fori_loop(0, PARTS, second_norm, 0, unroll=4)
    upper_ref[...] = dot(two_ref[...], up_ref[...])
    gact_ref[...] = dot(cot_ref[...], down_ref[...]).astype(BF)
    step = 32

    def gelu(chunk, carry):
        rows = pl.ds(pl.multiple_of(chunk * step, step), step)
        upper = upper_ref[rows, :]
        cdf = 0.5 + 0.5 * lax.erf(upper * math.sqrt(0.5))
        pdf = jnp.exp(upper * upper * -0.5) * (1.0 / math.sqrt(2.0 * math.pi))
        act_ref[rows, :] = (upper * cdf).astype(BF)
        gup_ref[rows, :] = (gact_ref[rows, :].astype(F32) * (cdf + upper * pdf)).astype(BF)
        return carry

    lax.fori_loop(0, TOKENS // step, gelu, 0)
    gres_ref[...] = dot_rt(gup_ref[...], up_ref[...])

    def second_back(part, carry):
        rows = rows_of(part)
        unit, inverse = unit_two_ref[rows, :], inverse_two_ref[rows, :]
        grad = gres_ref[rows, :].astype(BF).astype(F32)
        grad = cot_ref[rows, :].astype(F32) + normal_back(unit, inverse, grad)
        gres_ref[rows, :] = grad
        gmix_ref[rows, :] = grad.astype(BF)
        return carry

    lax.fori_loop(0, PARTS, second_back, 0, unroll=4)
    gatt_ref[...] = dot_rt(gmix_ref[...], proj_ref[...]).astype(BF)
    ds_ref[...] = jnp.zeros(ds_ref.shape, F32)

    def attend_back(part, carry):
        rows = rows_of(part)
        query, key, value = q_ref[rows, :], k_ref[rows, :], v_ref[rows, :]
        gatt = gatt_ref[rows, :]
        level = part % 2
        key_t = jnp.transpose(key)
        chunks = [slice(head * WIN, (head + 1) * WIN) for head in range(HEADS)]
        gowns = [gatt * mask for mask in half_masks]
        gprobs = [dot_rt(value, gown) for gown in gowns]
        gscores = []
        for head, chunk in enumerate(chunks):
            weight = prob_ref[part, chunk, :].astype(F32)
            gscore = weight * (gprobs[head] - jnp.sum(weight * gprobs[head], axis=0, keepdims=True))
            ds_ref[level, chunk, :] += gscore
            gscores.append(gscore.astype(BF))
        gkey = jnp.zeros((WIN, C), F32)
        gvalue = jnp.zeros((WIN, C), F32)
        for head, chunk in enumerate(chunks):
            own = slice(head * HEAD, (head + 1) * HEAD)
            turned_ref[own, :] = dot(key_t[own], gscores[head])
            gkey = gkey + dot(gscores[head], query * half_masks[head])
            gvalue = gvalue + dot(prob_ref[part, chunk, :], gowns[head])
        dq_ref[rows, :] = (jnp.transpose(turned_ref[...]) * SCALE).astype(BF)
        dk_ref[rows, :] = (gkey * SCALE).astype(BF)
        dv_ref[rows, :] = gvalue.astype(BF)
        return carry

    lax.fori_loop(0, PARTS, attend_back, 0, unroll=4)
    first = core_ref[0] == 0

    def put(start, zero, one):
        rows = slice(start, start + zero.shape[0])
        mine_ref[rows, :] = jnp.where(first, zero, one)
        other_ref[rows, :] = jnp.where(first, one, zero).astype(BF)

    gup = dot_lt(two_ref[...], gup_ref[...])
    gdown = dot_lt(cot_ref[...], act_ref[...])
    for chunk in range(6):
        columns = slice(chunk * LANES, (chunk + 1) * LANES)
        put(chunk * C, gup[:, columns], gdown[:, columns])
    normed = normed_ref[...]
    gq = dot_lt(normed, dq_ref[...])
    gk = dot_lt(normed, dk_ref[...])
    gv = dot_lt(normed, dv_ref[...])
    gproj = dot_lt(att_ref[...], gmix_ref[...])
    put(6 * C, gq[:, :LANES], gproj[:, :LANES])
    put(7 * C, gk[:, :LANES], jnp.concatenate([gq[:, LANES:], gk[:, LANES:]], axis=1))
    put(8 * C, gv[:, :LANES], jnp.concatenate([gv[:, LANES:], gproj[:, LANES:]], axis=1))
    mine_ref[9 * C :, :] = jnp.zeros((PACKED - 9 * C, LANES), F32)
    other_ref[9 * C :, :] = jnp.zeros((PACKED - 9 * C, LANES), BF)

    row = lax.broadcasted_iota(jnp.int32, (2 * WA, WIDE), 0)

    def table_grad(level, head):
        scores = jnp.transpose(ds_ref[level, head * WIN : (head + 1) * WIN, :])
        total = jnp.zeros((2 * WA, WIDE), F32)
        for pair in range(WO // 2):
            turn = (WO - 2 - 2 * pair) * WA
            block = scores[pair * 2 * WA : (pair + 1) * 2 * WA]
            block = jnp.concatenate([block, jnp.zeros((2 * WA, WIDE - WIN), F32)], axis=1)
            total = total + (pltpu.roll(block, turn, 1) if turn else block)
        total = jnp.where(row < WA, pltpu.roll(total, WA, 1), total)
        return total + pltpu.roll(total, WA, 0)

    for level in range(2):
        left = jnp.zeros((2 * WA, LANES), F32)
        for pair in range(HEADS // 2):
            both = jnp.where(row < WA, table_grad(level, 2 * pair), table_grad(level, 2 * pair + 1))
            start = pair * 2 * WA
            bsum_ref[level, start : start + 2 * WA, :] = both[:, :LANES]
            bsum_ref[level, MAIN + start : MAIN + start + 2 * WA, :] = both[:, LANES : 2 * LANES]
            rest = both[:, 2 * LANES :]
            left = left + (pltpu.roll(rest, pair * LEFT, 1) if pair else rest)
        bsum_ref[level, 2 * MAIN : 2 * MAIN + 2 * WA, :] = left
        bsum_ref[level, 2 * MAIN + 2 * WA :, :] = jnp.zeros((BIAS_ROWS - 2 * MAIN - 2 * WA, LANES), F32)
    gbias_ref[...] = bsum_ref[...].reshape(2 * BIAS_ROWS, LANES).astype(BF)


def added(one, two):
    return (one.astype(F32) + two.astype(F32)).astype(BF)


def first_kernel(mine_ref, got_ref, own_ref, came_ref, wait_ref, sum_ref, bias_ref):
    sum_ref[...] = (mine_ref[...] + got_ref[...].astype(F32)).astype(BF)
    bias_ref[...] = added(own_ref[...], came_ref[...])


def middle_kernel(got_ref, own_ref, came_ref, wait_ref, wide_ref, bias_ref):
    total = jnp.sum(got_ref[...].astype(F32), axis=0).astype(BF)
    for block in range(wide_ref.shape[0]):
        wide_ref[block] = total
    bias_ref[...] = added(own_ref[...], came_ref[...])


def late_kernel(
    act_ref, res_ref, gres_ref, dq_ref, dk_ref, dv_ref, unit_ref, inverse_ref, qkv_ref, down_ref, order_ref,
    own_ref, above_ref, beside_ref, corner_ref, grad_ref,
):
    result = (res_ref[...] + dot_rt(act_ref[...], down_ref[...])).astype(BF)
    grads = (dq_ref, dk_ref, dv_ref)
    grad_ref[...] = sum(dot_rt(ref[...], qkv_ref[:, i * C : (i + 1) * C]) for i, ref in enumerate(grads))

    def first_back(part, carry):
        rows = pl.ds(pl.multiple_of(part * WIN, WIN), WIN)
        grad = grad_ref[rows, :].astype(BF).astype(F32)
        grad_ref[rows, :] = gres_ref[rows, :] + normal_back(unit_ref[rows, :], inverse_ref[rows, :], grad)
        return carry

    lax.fori_loop(0, PARTS, first_back, 0, unroll=4)
    order = order_ref[...]
    rows = jnp.concatenate([dot(order, result), dot(order, grad_ref[...].astype(BF))], axis=1)
    start = 0
    for ref in (own_ref, above_ref, beside_ref, corner_ref):
        ref[...] = rows[start : start + ref.shape[0]].astype(BF)
        start += ref.shape[0]


def join_kernel(own_ref, above_ref, beside_ref, corner_ref, order_ref, result_ref, gtok_ref):
    pieces = [ref[...].astype(F32) for ref in (own_ref, above_ref, beside_ref, corner_ref)]
    rows = dot(order_ref[...], jnp.concatenate(pieces, axis=0).astype(BF))
    for array, ref in enumerate((result_ref, gtok_ref)):
        part = rows[:, array * C : (array + 1) * C]
        for level in range(2):
            for row in range(WA):
                at = (level * WA + row) * 2 * WO
                ref[level, row] = part[at : at + 2 * WO].astype(BF)


def final_kernel(
    count, core_ref, mine_ref, other_ref, gbias_ref, back_ref,
    qkv_ref, proj_ref, up_ref, down_ref, bias_ref,
):
    first = core_ref[0] == 0
    squares = jnp.zeros((C, LANES), F32)
    for place in range(9):
        for ref in (mine_ref, other_ref):
            part = ref[place * C : (place + 1) * C, :].astype(F32)
            squares = squares + part * part
    total = jnp.sum(squares)
    factor = jnp.minimum(1.0, math.sqrt(count) / (jnp.sqrt(jnp.full((8, LANES), total)) + 1e-06))[:1]

    def chunk(half, place):
        rows = slice(place * C, (place + 1) * C)
        mine, other = mine_ref[rows, :].astype(F32), other_ref[rows, :].astype(F32)
        return (jnp.where(first, other, mine) if half else jnp.where(first, mine, other)) * factor

    for place in range(6):
        up_ref[:, place * LANES : (place + 1) * LANES] = chunk(0, place)
        down_ref[:, place * LANES : (place + 1) * LANES] = chunk(1, place)
    last = C - LANES
    left, right = chunk(1, 7), chunk(1, 8)
    qkv_ref[:, :C] = jnp.concatenate([chunk(0, 6), left[:, :last]], axis=1)
    qkv_ref[:, C : 2 * C] = jnp.concatenate([chunk(0, 7), left[:, last:]], axis=1)
    qkv_ref[:, 2 * C :] = jnp.concatenate([chunk(0, 8), right[:, :last]], axis=1)
    proj_ref[...] = jnp.concatenate([chunk(1, 6), right[:, last:]], axis=1)

    sums = gbias_ref[...].astype(F32)
    tables = []
    for level in range(2):
        packed = sums[level * BIAS_ROWS : (level + 1) * BIAS_ROWS]
        left = packed[2 * MAIN : 2 * MAIN + 2 * WA]
        left = [left] + [pltpu.roll(left, LANES - pair * LEFT, 1) for pair in range(1, HEADS // 2)]
        rows = [packed[:MAIN], packed[MAIN : 2 * MAIN], jnp.concatenate(left, axis=0)]
        rows = jnp.concatenate(rows, axis=1).astype(BF)
        tables.append(dot(rows, back_ref[level]) * factor[:, :1])
    row = lax.broadcasted_iota(jnp.int32, (2 * WA, 2 * CUT), 0)
    for pair in range(HEADS // 2):
        upper, lower = [table[pair * 2 * WA : (pair + 1) * 2 * WA] for table in tables]
        bias_ref[0, 0, 2 * pair] = jnp.where(row < WA, upper, pltpu.roll(lower, WA, 0))
        bias_ref[0, 0, 2 * pair + 1] = jnp.where(row < WA, pltpu.roll(upper, WA, 0), lower)


def call(kernel, outs, scalars, arrays, scratch=(), limit=SMALL):
    spaces = [pl.BlockSpec(memory_space=pltpu.SMEM)] * scalars
    spaces += [pl.BlockSpec(memory_space=pltpu.VMEM)] * arrays
    return pl.pallas_call(
        kernel,
        out_shape=outs,
        in_specs=spaces,
        out_specs=[pl.BlockSpec(memory_space=pltpu.VMEM)] * len(outs),
        scratch_shapes=scratch,
        compiler_params=pltpu.CompilerParams(vmem_limit_bytes=limit),
    )


def shape(*sizes, kind=F32):
    return jax.ShapeDtypeStruct(sizes, kind)


def from_next(block, axes, distance):
    sizes = [lax.axis_size(axis) for axis in axes]
    route = []
    for place in np.ndindex(*sizes):
        source = [(i + distance) % size for i, size in zip(place, sizes)]
        route.append((int(np.ravel_multi_index(source, sizes)), int(np.ravel_multi_index(place, sizes))))
    return lax.ppermute(block, tuple(axes), route)


def roll_back_start(*arrays):
    outs = [shape(rows, 2 * C, kind=BF) for rows in (LONG, LONG, SHORT, SHORT)]
    order = jnp.asarray(split_order(), BF)
    pieces = call(late_kernel, outs, 0, 11, [pltpu.VMEM((TOKENS, C), F32)])(*arrays, order)
    own, above, beside, corner = pieces
    above = from_next(above, ["lat"], -1)
    corner = from_next(corner, ["lat", "lon"], -1)
    beside = from_next(beside, ["lon"], -1)
    return own, above, beside, corner


def roll_back_end(pieces):
    whole = shape(2, WA, 2 * WO, C, kind=BF)
    return call(join_kernel, [whole, whole], 0, 5)(*pieces, jnp.asarray(join_order(), BF))


def gradient_sums(mine, other, bias, pieces):
    lat, lon = lax.axis_size("lat"), lax.axis_size("lon")
    half, depth = lat // 2, lon // 2
    pairs = [(i, i ^ 1) for i in range(lat)]
    planes = [
        [(2 * i + core) * lon + 2 * z + low for i in range(half) for low in range(2)]
        for core in range(2)
        for z in range(depth)
    ]
    columns = [[2 * z + low for z in range(depth)] for low in range(2)]
    share = PACKED // lat

    def partner(block, distance):
        return lax.ppermute(block, "lon", [(i, i ^ distance) for i in range(lon)])

    def middle(got, own, came, blocks, wait):
        outs = [shape(blocks, share, LANES, kind=BF), shape(2 * BIAS_ROWS, LANES, kind=BF)]
        return call(middle_kernel, outs, 0, 4)(got, own, came, wait)

    own, above, beside, corner = pieces
    outs = [shape(PACKED, LANES, kind=BF), shape(2 * BIAS_ROWS, LANES, kind=BF)]
    got = lax.ppermute(other, "lat", pairs)
    mine, bias = call(first_kernel, outs, 0, 5)(mine, got, bias, partner(bias, 2), own[:8, :LANES])
    got = lax.all_to_all(mine.reshape(lat, share, LANES), ("lat", "lon"), 0, 0, axis_index_groups=planes)
    wide, bias = middle(got, bias, partner(bias, 4), depth, corner[:8, :LANES])
    got = lax.all_to_all(wide, "lon", 0, 0, axis_index_groups=columns)
    wide, bias = middle(got, bias, partner(bias, 1), lat, above[:8, :LANES])
    bias = added(bias, partner(bias, 8))
    mine = lax.all_to_all(wide, ("lat", "lon"), 0, 0, axis_index_groups=planes)
    wait = added(bias[:8], beside[:8, :LANES])
    mine = lax.dynamic_update_slice(mine, wait[None], (lat - 1, share - 8, 0))
    other = lax.ppermute(mine, "lat", pairs)
    return mine.reshape(PACKED, LANES), other.reshape(PACKED, LANES), bias


def on_device(tokens, w_qkv, w_proj, w_up, w_down, earth_bias, cotangent):
    band = lax.axis_index("lat")
    bands = lax.axis_size("lat")
    core = (band % 2).astype(jnp.int32).reshape(1)
    last = (band == bands - 1).astype(jnp.int32).reshape(1)

    wide, narrow = shape(2, 2, HALF, 2 * WO, C, kind=BF), shape(2, 2, HALF, 8, C, kind=BF)
    below, beside, corner = call(halo_kernel, [wide, narrow, narrow], 0, 2)(tokens, cotangent)
    below = from_next(below, ["lat"], 1)
    corner = from_next(corner, ["lat", "lon"], 1)
    beside = from_next(beside, ["lon"], 1)
    back = table_back()
    bias = call(bias_kernel, [shape(2, HEADS * WIN, WIN)], 1, 1)(last, earth_bias)[0]

    def tokens_of(width, kind=BF):
        return pltpu.VMEM((TOKENS, width), kind)

    outs = [shape(PACKED, LANES), shape(PACKED, LANES, kind=BF), shape(2 * BIAS_ROWS, LANES, kind=BF)]
    outs += [shape(TOKENS, HID, kind=BF), shape(TOKENS, C), shape(TOKENS, C)]
    outs += [shape(TOKENS, C, kind=BF)] * 3 + [shape(TOKENS, C)] * 2
    scratch = [pltpu.VMEM((SOURCES, C), F32)] + [tokens_of(C)] * 6
    scratch += [pltpu.VMEM((PARTS, HEADS * WIN, WIN), BF), tokens_of(C), tokens_of(C), tokens_of(HID, F32)]
    scratch += [tokens_of(HID)] * 2 + [tokens_of(C)] * 2 + [pltpu.VMEM((2, HEADS * WIN, WIN), F32)]
    scratch += [pltpu.VMEM((2, BIAS_ROWS, LANES), F32), pltpu.VMEM((C, WIN), F32)] + [tokens_of(C, F32)] * 3
    mine, other, grad_table, *late = call(block_kernel, outs, 1, 11, scratch, limit=LARGE)(
        core, tokens, cotangent, below, beside, corner, jnp.asarray(window_order(), BF),
        w_qkv, w_proj, w_up, w_down.T, bias,
    )
    pieces = roll_back_start(*late, w_qkv, w_down.T)
    sums = gradient_sums(mine, other, grad_table, pieces)
    result, grad_tokens = roll_back_end(pieces)

    count = w_qkv.size + w_proj.size + w_up.size + w_down.size + earth_bias.size * bands
    outs = [shape(C, 3 * C), shape(C, C), shape(C, HID), shape(C, HID), shape(1, 1, HEADS, 2 * WA, 2 * CUT)]
    grads = call(functools.partial(final_kernel, count), outs, 1, 4)(core, *sums, jnp.asarray(back, BF))
    return (result, grad_tokens, *grads[:3], grads[3].T, grads[4])


def solution(mesh):
    placed = (
        P(None, "lat", "lon", None),
        P(),
        P(),
        P(),
        P(),
        P("lat", None, None, None, None),
        P(None, "lat", "lon", None),
    )
    return jax.shard_map(
        on_device,
        mesh=mesh,
        in_specs=placed,
        out_specs=(
            P(None, "lat", "lon", None),
            P(None, "lat", "lon", None),
            P(),
            P(),
            P(),
            P(),
            P("lat", None, None, None, None),
        ),
        check_vma=False,
    )
```
